256 devices in a mesh: samp: 8 (over z_hi, core), grp: 32 (over z_lo, x, y).
Axes of the slice: x: 4, y: 4, z: 8 (z_hi: 4, z_lo: 2; z = z_hi * 2 + z_lo), core: 2. Of those that a mesh axis runs over, the one named last changes fastest.
Arguments:
- volumes: bfloat16 [8, 64, 128, 16, 128], P('samp', None, 'grp'), may hold values from -6 to 6
- w_first: bfloat16 [128, 1728], replicated, may hold values from -0.15625 to 0.15625
- bias_first: float32 [128], replicated, may hold values from -4 to 4
- w_second: bfloat16 [256, 27, 128], replicated, may hold values from -0.109375 to 0.109375
- cotangent: bfloat16 [8, 256, 32, 128], P('samp', 'grp'), may hold values from -6 to 6
Outputs:
- pre_grad: bfloat16 [8, 128, 64, 4, 128], P('samp', None, 'grp')
- w2_grad: float32 [256, 27, 128], P(None, None, 'grp')
The draws below stay inside these ranges and needn't reach their ends.
All inputs are finite; a program needn't handle non-finite values.
Results may differ from the reference program's by a relative error of at most 0.0049.
Values may be sent and summed in bfloat16 or wider, within the bound.
A program may use at most 64 MiB of HBM per device.

```python
import math
import jax
import jax.numpy as jnp
from jax import lax

CIN = 64
CH1 = 128
FILT = 256
YCELLS = 32
ZCELLS = 64
SAMPLES = 8
XCELLS = 128
X1 = 64
Y1 = 16
Z1 = 32
X2 = 32
Y2 = 8
Z2 = 16


def level_of(own_key, shape, cuts, smallest, largest):
    loudness = 1.0
    for position, blocks in cuts:
        steps = jax.random.uniform(jax.random.fold_in(jax.random.fold_in(own_key, 6), position), (blocks,), jnp.float32, smallest / len(cuts), largest / len(cuts))
        loudness = loudness * jnp.repeat(jnp.exp(steps), shape[position] // blocks).reshape((-1,) + (1,) * (len(shape) - 1 - position))
    return loudness


def scatter_about(own_key, extent, spread, limit, shards=(), dtype=jnp.bfloat16):
    array = spread * jax.random.normal(own_key, extent, jnp.float32)
    if shards:
        array = array * level_of(own_key, extent, shards, -0.22, 0.18)
    return jnp.clip(array, -limit, limit).astype(dtype)


def setup_inputs(seed: int = 0) -> dict:
    arg_keys = jax.random.split(jax.random.key(seed), 6)
    volumes = scatter_about(arg_keys[0], (SAMPLES, CIN, XCELLS, 16, Y2 * Z2), 1.0, 6.0, ((0, 8), (2, 32)))
    w_first = scatter_about(arg_keys[1], (CH1, 27 * CIN), (27 * CIN) ** -0.5, 0.15625)
    bias_first = scatter_about(arg_keys[2], (CH1,), 1.0, 4.0, (), jnp.float32)
    w_second = scatter_about(arg_keys[3], (FILT, 27, CH1), (27 * CH1) ** -0.5, 0.109375)
    cotangent = scatter_about(arg_keys[4], (SAMPLES, FILT, X2, Y2 * Z2), 1.0, 6.0, ((0, 8), (1, 32)))
    return {"volumes": volumes, "w_first": w_first, "bias_first": bias_first, "w_second": w_second, "cotangent": cotangent}


OFFSETS = (-1, 0, 1)

def strided_tap(volume, offset_x, offset_y, offset_z):
    rolled = jnp.roll(volume, (-offset_x, -offset_y, -offset_z), axis=(1, 2, 3))
    return rolled[:, ::2, ::2, ::2]

def natural_input(volume):
    split = volume.reshape(CIN, XCELLS, 4, 4, Y2, Z2)
    return jnp.transpose(split, (0, 1, 4, 2, 5, 3)).reshape(CIN, XCELLS, YCELLS, ZCELLS)

def phase_output(field):
    split = field.reshape(CH1, X1, Y2, 2, Z2, 2)
    return jnp.transpose(split, (0, 1, 3, 5, 2, 4)).reshape(CH1, X1, 4, Y2 * Z2)

def reference(volumes, w_first, bias_first, w_second, cotangent):

    def one_sample(sample_pair):
        volume, cotan = sample_pair
        volume = natural_input(volume)
        total = jnp.zeros((CH1, X1 * Y1 * Z1), jnp.float32)
        tap_index = 0
        for offset_x in OFFSETS:
            for offset_y in OFFSETS:
                for offset_z in OFFSETS:
                    patch = strided_tap(volume, offset_x, offset_y, offset_z).reshape(CIN, -1)
                    weights = w_first[:, tap_index * CIN:(tap_index + 1) * CIN]
                    total = total + jnp.dot(weights, patch, preferred_element_type=jnp.float32)
                    tap_index += 1
        pre_act = total + bias_first[:, None]
        act = jax.nn.silu(pre_act).astype(jnp.bfloat16).reshape(CH1, X1, Y1, Z1)
        cotan_flat = cotan.reshape(FILT, -1)
        act_grad = jnp.zeros((CH1, X1, Y1, Z1), jnp.float32)
        weight_grads = []
        tap_index = 0
        for offset_x in OFFSETS:
            for offset_y in OFFSETS:
                for offset_z in OFFSETS:
                    patch = strided_tap(act, offset_x, offset_y, offset_z).reshape(CH1, -1)
                    weight_grads.append(jnp.dot(cotan_flat, patch.T, preferred_element_type=jnp.float32))
                    product = jnp.dot(w_second[:, tap_index, :].T, cotan_flat, preferred_element_type=jnp.float32)
                    placed = jnp.zeros((CH1, X1, Y1, Z1), jnp.float32)
                    placed = placed.at[:, ::2, ::2, ::2].set(product.reshape(CH1, X2, Y2, Z2))
                    act_grad = act_grad + jnp.roll(placed, (offset_x, offset_y, offset_z), axis=(1, 2, 3))
                    tap_index += 1
        act_grad = act_grad.astype(jnp.bfloat16).reshape(CH1, -1)
        sigmoid_pre = jax.nn.sigmoid(pre_act)
        slope = sigmoid_pre * (1.0 + pre_act * (1.0 - sigmoid_pre))
        pre_grad = (act_grad.astype(jnp.float32) * slope).astype(jnp.bfloat16)
        return (phase_output(pre_grad.reshape(CH1, X1, Y1, Z1)), jnp.stack(weight_grads, axis=1))
    pre_grads, weight_parts = lax.map(one_sample, (volumes, cotangent))
    scale = 1.0 / math.sqrt(SAMPLES * X2 * Y2 * Z2)
    w2_grad = lax.optimization_barrier(jnp.sum(weight_parts, axis=0)) * scale
    return (pre_grads, w2_grad)
```

```python
import functools
import math

import jax
import jax.numpy as jnp
from jax import lax
from jax.experimental import pallas as pl
from jax.experimental.pallas import tpu as pltpu
from jax.sharding import PartitionSpec as P

MESH = pl.DeviceIdType.MESH
F32 = jnp.float32
BF16 = jnp.bfloat16

CIN = 64
CH = 128
FILT = 256
HALF = 128
LANES = 128
ZQ = 16
GRP = 32
SAMP = 8
TAPS = 27
COMBOS = [(b, e) for b in (-1, 0, 1) for e in (-1, 0, 1)]
PHASES = [(0, 0), (0, 1), (1, 0), (1, 1)]
TAP_ORDER = [t for n in range(9) for t in (18 + n, n)] + [9 + n for n in range(9)]
SLOTS = 28
ROWS_A = 64
ROWS_B = 48
ROWS = ROWS_A + ROWS_B


def lane_index(shape):
    return lax.broadcasted_iota(jnp.int32, shape, len(shape) - 1)


def y_before(x):
    return pltpu.roll(x, ZQ, 1)


def z_before(x):
    first = lane_index(x.shape) % ZQ == 0
    return jnp.where(first, pltpu.roll(x, LANES + 1 - ZQ, 1), pltpu.roll(x, 1, 1))


def row_y_after(x):
    return jnp.concatenate([x[ZQ:], x[:ZQ]], axis=0)


def row_z_after(x):
    rows = x.shape[0]
    last = lax.broadcasted_iota(jnp.int32, x.shape, 0) % ZQ == ZQ - 1
    return jnp.where(last, pltpu.roll(x, ZQ - 1, 0), pltpu.roll(x, rows - 1, 0))


def kernel(
    vol, w1t, bias, w2, cot,
    pre_out, w2_out,
    vbuf, w1tv, w1s, biasv, w2v, cotv, cstg, cstage, crecv, cotf, cpart,
    perm, tn, ty, tz, tyz, pre_s, act_own, act_part, carry, send_buf, recv_buf,
    acc_s, zrecv, fin, cvar, pgf,
    lsem, vsem, halo_sem, cot_sem, cx_sem, act_sem, rs_sem, z_sem, ag_sem,
):
    me = lax.axis_index("grp")
    samp = lax.axis_index("samp")
    core = lax.rem(samp, 2)
    zhi = lax.div(samp, 2)
    other = samp + 1 - 2 * core

    ld_cot = pltpu.make_async_copy(cot, cotv, lsem.at[0])
    ld_w1 = pltpu.make_async_copy(w1t, w1tv, lsem.at[1])
    ld_bias = pltpu.make_async_copy(bias, biasv, lsem.at[2])
    ld_w2 = pltpu.make_async_copy(w2, w2v, lsem.at[3])
    ld_vol = [pltpu.make_async_copy(vol.at[:, x], vbuf.at[x + 1], vsem.at[x]) for x in range(4)]
    ld_cot.start()
    ld_w1.start()
    ld_bias.start()
    for x in (1, 2, 3, 0):
        ld_vol[x].start()
    ld_w2.start()

    barrier = pltpu.get_barrier_semaphore()

    def greet_grp(k, _):
        pl.semaphore_signal(
            barrier, inc=1, device_id={"grp": lax.rem(me + k, GRP)}, device_id_type=MESH
        )
        return 0

    def greet_samp(k, _):
        pl.semaphore_signal(
            barrier, inc=1, device_id={"samp": lax.rem(samp + k, SAMP)}, device_id_type=MESH
        )
        return 0

    lax.fori_loop(1, GRP, greet_grp, 0)
    lax.fori_loop(1, SAMP, greet_samp, 0)

    ld_cot.wait()
    for f in range(8):
        x = cotv[f].astype(F32)
        cstg[pl.ds(f, GRP, stride=16), :] = x
        cstg[pl.ds(8 + f, GRP, stride=16), :] = jnp.concatenate([x[1:], x[:1]], axis=0)
    cstage[...] = cstg[...].reshape(GRP, 16, LANES).astype(BF16)

    pl.semaphore_wait(barrier, GRP - 1 + SAMP - 1)

    halo = pltpu.make_async_remote_copy(
        src_ref=vol.at[:, 3], dst_ref=vbuf.at[0],
        send_sem=halo_sem.at[0], recv_sem=halo_sem.at[1],
        device_id={"grp": lax.rem(me + 1, GRP)}, device_id_type=MESH,
    )

    def send_cot(k, _):
        dest = lax.rem(me + k, GRP)
        pltpu.make_async_remote_copy(
            src_ref=cstage.at[dest], dst_ref=crecv.at[me],
            send_sem=cot_sem.at[0], recv_sem=cot_sem.at[1],
            device_id={"grp": dest}, device_id_type=MESH,
        ).start()
        return 0

    lax.fori_loop(1, GRP, send_cot, 0)
    halo.start()
    crecv[me] = cstage[me]

    ld_w1.wait()
    ld_bias.wait()
    w1s[...] = jnp.transpose(w1tv[...])
    bias_rows = jnp.transpose(jnp.broadcast_to(biasv[...], (CH, CH)))
    row = lax.broadcasted_iota(jnp.int32, (256, 256), 0)
    col = lax.broadcasted_iota(jnp.int32, (256, 256), 1)
    perm[...] = jnp.where(col == (row % 16) * 16 + row // 16, 1.0, 0.0).astype(BF16)

    def by_phase(x):
        for blk in range(4):
            rows = vbuf[x, 16 * blk : 16 * blk + 16].reshape(256, LANES)
            moved = jnp.dot(perm[...], rows, preferred_element_type=F32)
            here = slice(16 * blk, 16 * blk + 16)
            tn[x, :, here, :] = moved.reshape(16, 16, LANES).astype(BF16)
            ty[x, :, here, :] = y_before(moved[192:256]).reshape(4, 16, LANES).astype(BF16)
            ends = jnp.concatenate([moved[64 * r + 48 : 64 * r + 64] for r in range(4)], axis=0)
            ends = z_before(ends)
            tz[x, :, here, :] = ends.reshape(4, 16, LANES).astype(BF16)
            tyz[x, here, :] = y_before(ends[48:64]).astype(BF16)

    def patch(x, qy, qz, b, e):
        along_y, along_z = 2 * qy + b, 2 * qz + e
        ry, rz = along_y % 4, along_z % 4
        if along_y < 0 and along_z < 0:
            return tyz[x]
        if along_y < 0:
            return ty[x, rz]
        if along_z < 0:
            return tz[x, ry]
        return tn[x, 4 * ry + rz]

    def first_layer(i):
        for pair in (0, 1):
            columns = []
            for q in (2 * pair, 2 * pair + 1):
                qy, qz = PHASES[q]
                columns.append(
                    jnp.concatenate(
                        [patch(2 * i + a, qy, qz, b, e) for a in range(3) for b, e in COMBOS], axis=0
                    )
                )
            patches = jnp.concatenate(columns, axis=1)
            pre = jnp.dot(w1s[...], patches, preferred_element_type=F32)
            for h in (0, 1):
                part = pre[:, LANES * h : LANES * (h + 1)] + bias_rows
                pre_s[i, 2 * pair + h] = part
                act_own[i, 2 * pair + h] = (part / (1.0 + jnp.exp(-part))).astype(BF16)

    def exchange_act(i):
        return pltpu.make_async_remote_copy(
            src_ref=act_own.at[i], dst_ref=act_part.at[i],
            send_sem=act_sem.at[0, i], recv_sem=act_sem.at[1, i],
            device_id={"samp": other}, device_id_type=MESH,
        )

    for x in (1, 2, 3):
        ld_vol[x].wait()
        by_phase(x + 1)
    first_layer(1)
    act_copy = [exchange_act(0), exchange_act(1)]
    act_copy[1].start()

    pltpu.make_async_copy(
        crecv.at[pl.ds(0, GRP - 1)], crecv.at[pl.ds(0, GRP - 1)], cot_sem.at[1]
    ).wait()
    got = crecv[...].astype(F32)
    for p in (0, 1):
        cotf[p] = got[:, 8 * p : 8 * p + 8].reshape(FILT, LANES).astype(BF16)
    cx = pltpu.make_async_remote_copy(
        src_ref=cotf.at[:, pl.ds(pl.multiple_of(HALF * (1 - core), HALF), HALF), :], dst_ref=cpart,
        send_sem=cx_sem.at[0], recv_sem=cx_sem.at[1],
        device_id={"samp": other}, device_id_type=MESH,
    )
    cx.start()

    ld_vol[0].wait()
    by_phase(1)

    my_half = pl.ds(pl.multiple_of(HALF * core, HALF), HALF)

    def second_patch(i, n):
        b, e = COMBOS[n]
        phase = 2 * (b != 0) + (e != 0)
        parts = []
        for ref in (act_own, act_part):
            x = ref[i, phase]
            if b < 0 or e < 0:
                x = x.astype(F32)
                if e < 0:
                    x = z_before(x)
                if b < 0:
                    x = y_before(x)
                x = x.astype(BF16)
            parts.append(x)
        return jnp.concatenate(parts, axis=1)

    contract = (((1,), (1,)), ((), ()))

    def pack(group, taps):
        low = lax.broadcasted_iota(jnp.int32, (16, 8, LANES), 1) < 4
        t = [x.reshape(16, 8, LANES) for x in taps]
        turned = [pltpu.roll(x, 4, 1) for x in t]
        even = [jnp.where(low, t[j], turned[j + 1]) for j in (0, 2)]
        odd = [jnp.where(low, turned[j], t[j + 1]) for j in (0, 2)]
        rows = slice(16 * group, 16 * group + 16)
        send_buf[:, 0, rows, :] = jnp.concatenate(even, axis=1).astype(BF16)
        send_buf[:, 1, rows, :] = jnp.concatenate(odd, axis=1).astype(BF16)

    def send_chunk(which):
        rows = pl.ds(0, ROWS_A) if which == 0 else pl.ds(ROWS_A, ROWS_B)

        def body(k, _):
            dest = lax.rem(me + k, GRP)
            pltpu.make_async_remote_copy(
                src_ref=send_buf.at[lax.div(dest, 2), lax.rem(dest, 2), rows],
                dst_ref=recv_buf[which].at[k - 1],
                send_sem=rs_sem.at[0, which], recv_sem=rs_sem.at[1, which],
                device_id={"grp": dest}, device_id_type=MESH,
            ).start()
            return 0

        lax.fori_loop(1, GRP, body, 0)

    def cot_rhs(p):
        return jnp.concatenate([cotf[p, my_half, :], cpart[p]], axis=1)

    act_copy[1].wait_recv()
    cx.wait_recv()
    rhs_both = jnp.concatenate([cot_rhs(0), cot_rhs(1)], axis=0)
    held = []
    for n in range(9):
        d = lax.dot_general(second_patch(1, n), rhs_both, contract, preferred_element_type=F32)
        held += [d[:, :LANES], d[:, LANES:]]
        if len(held) == 4:
            pack(n // 2, held)
            held = []
    carry[0] = held[0]
    carry[1] = held[1]
    send_chunk(0)

    halo.wait_recv()
    by_phase(0)
    first_layer(0)
    act_copy[0].start()

    for p in (0, 1):
        turned = jnp.transpose(cotf[p].astype(F32))
        cvar[p, 0] = turned.astype(BF16)
        cvar[p, 2] = row_y_after(turned).astype(BF16)
        after = row_z_after(turned)
        cvar[p, 1] = after.astype(BF16)
        cvar[p, 3] = row_y_after(after).astype(BF16)

    act_copy[0].wait_recv()
    rhs_one = cot_rhs(0)
    held = [carry[0], carry[1]]
    group = 4
    for n in range(9):
        held.append(
            lax.dot_general(second_patch(0, n), rhs_one, contract, preferred_element_type=F32)
        )
        if len(held) == 4:
            pack(group, held)
            group += 1
            held = []
    pack(group, held + [jnp.zeros((CH, LANES), F32)] * (4 - len(held)))
    send_chunk(1)

    ld_w2.wait()
    for i in (0, 1):
        for q, (qy, qz) in enumerate(PHASES):
            left, right = [], []
            for a, p in ((0, 0),) if i == 0 else ((1, 0), (-1, 1)):
                for b, sy in ((0, 0),) if qy == 0 else ((1, 0), (-1, 1)):
                    for e, sz in ((0, 0),) if qz == 0 else ((1, 0), (-1, 1)):
                        left.append(cvar[p, 2 * sy + sz])
                        right.append(w2v[9 * (a + 1) + 3 * (b + 1) + e + 1])
            grad = jnp.dot(
                jnp.concatenate(left, axis=1),
                jnp.concatenate(right, axis=0),
                preferred_element_type=F32,
            )
            grad = jnp.transpose(grad.astype(BF16).astype(F32))
            z = pre_s[i, q]
            g = 1.0 / (1.0 + jnp.exp(-z))
            pgf[pl.ds(4 * i + q, CH, stride=8), :] = grad * (g * (1.0 + z * (1.0 - g)))
    pre_out[...] = pgf[...].reshape(CH, 8, LANES).astype(BF16)

    mine = send_buf.at[lax.div(me, 2), lax.rem(me, 2)]
    for which, rows in ((0, pl.ds(0, ROWS_A)), (1, pl.ds(ROWS_A, ROWS_B))):
        pltpu.make_async_copy(recv_buf[which], recv_buf[which], rs_sem.at[1, which]).wait()
        acc_s[rows, :] = lax.fori_loop(
            0,
            GRP - 1,
            lambda j, acc: acc + recv_buf[which][j].astype(F32),
            mine[rows, :].astype(F32),
        )
    acc_s[pl.ds(ROWS, 128 - ROWS), :] = jnp.zeros((128 - ROWS, LANES), F32)

    def z_peer(k):
        return lax.rem(zhi + k, 4)

    z_copies = []
    for k in (1, 2, 3):
        peer = z_peer(k)
        z_copies.append(
            pltpu.make_async_remote_copy(
                src_ref=acc_s.at[pl.ds(pl.multiple_of(32 * peer, 32), 32)], dst_ref=zrecv.at[k - 1],
                send_sem=z_sem.at[0, k - 1], recv_sem=z_sem.at[1, k - 1],
                device_id={"samp": 2 * peer + core}, device_id_type=MESH,
            )
        )
        z_copies[-1].start()
    for c in z_copies:
        c.wait_recv()
    scale = 1.0 / math.sqrt(32768)
    my_rows = pl.ds(pl.multiple_of(32 * zhi, 32), 32)
    fin_rows = pl.ds(pl.multiple_of(128 * core + 32 * zhi, 32), 32)
    fin[fin_rows, :] = (acc_s[my_rows, :] + zrecv[0] + zrecv[1] + zrecv[2]) * scale

    def send_fin(k, _):
        pltpu.make_async_remote_copy(
            src_ref=fin.at[fin_rows], dst_ref=fin.at[fin_rows],
            send_sem=ag_sem.at[0], recv_sem=ag_sem.at[1],
            device_id={"samp": lax.rem(samp + k, SAMP)}, device_id_type=MESH,
        ).start()
        return 0

    lax.fori_loop(1, SAMP, send_fin, 0)
    seven = fin.at[pl.ds(0, 7 * 32)]
    pltpu.make_async_copy(seven, seven, ag_sem.at[1]).wait()
    for slot, tap in enumerate(TAP_ORDER):
        for h in (0, 1):
            w2_out[tap, :, LANES * h : LANES * (h + 1)] = fin[128 * h + 4 * slot : 128 * h + 4 * slot + 4, :]

    halo.wait_send()
    pltpu.make_async_copy(
        cstage.at[pl.ds(0, GRP - 1)], cstage.at[pl.ds(0, GRP - 1)], cot_sem.at[0]
    ).wait()
    cx.wait_send()
    for c in act_copy + z_copies:
        c.wait_send()
    for which in (0, 1):
        pltpu.make_async_copy(recv_buf[which], recv_buf[which], rs_sem.at[0, which]).wait()
    pltpu.make_async_copy(seven, seven, ag_sem.at[0]).wait()


def on_device(volumes, w_first, bias_first, w_second, cotangent):
    any_space = pl.BlockSpec(memory_space=pltpu.HBM)
    vmem = pl.BlockSpec(memory_space=pltpu.VMEM)
    dma = pltpu.SemaphoreType.DMA
    recv_a = pltpu.VMEM((GRP - 1, ROWS_A, LANES), BF16)
    recv_b = pltpu.VMEM((GRP - 1, ROWS_B, LANES), BF16)
    scratch = [
        pltpu.VMEM((5, CIN, 16, LANES), BF16),
        pltpu.VMEM((TAPS * CIN, CH), BF16),
        pltpu.VMEM((CH, TAPS * CIN), BF16),
        pltpu.VMEM((1, CH), F32),
        pltpu.VMEM((TAPS, FILT, CH), BF16),
        pltpu.VMEM((8, GRP, LANES), BF16),
        pltpu.VMEM((GRP * 16, LANES), F32),
        pltpu.VMEM((GRP, 16, LANES), BF16),
        pltpu.VMEM((GRP, 16, LANES), BF16),
        pltpu.VMEM((2, FILT, LANES), BF16),
        pltpu.VMEM((2, HALF, LANES), BF16),
        pltpu.VMEM((256, 256), BF16),
        pltpu.VMEM((5, 16, CIN, LANES), BF16),
        pltpu.VMEM((5, 4, CIN, LANES), BF16),
        pltpu.VMEM((5, 4, CIN, LANES), BF16),
        pltpu.VMEM((5, CIN, LANES), BF16),
        pltpu.VMEM((2, 4, CH, LANES), F32),
        pltpu.VMEM((2, 4, CH, LANES), BF16),
        pltpu.VMEM((2, 4, CH, LANES), BF16),
        pltpu.VMEM((2, CH, LANES), F32),
        pltpu.VMEM((GRP // 2, 2, ROWS, LANES), BF16),
        recv_a,
        recv_b,
        pltpu.VMEM((128, LANES), F32),
        pltpu.VMEM((3, 32, LANES), F32),
        pltpu.VMEM((2 * 128, LANES), F32),
        pltpu.VMEM((2, 4, LANES, FILT), BF16),
        pltpu.VMEM((CH * 8, LANES), F32),
        dma((4,)),
        dma((4,)),
        dma((2,)),
        dma((2,)),
        dma((2,)),
        dma((2, 2)),
        dma((2, 2)),
        dma((2, 3)),
        dma((2,)),
    ]

    def body(*refs):
        refs = list(refs)
        at = 7 + 20 + 1
        both = tuple(refs[at : at + 2])
        kernel(*refs[:at], both, *refs[at + 2 :])

    pre, w2g = pl.pallas_call(
        body,
        out_shape=(
            jax.ShapeDtypeStruct((CH, 8, LANES), BF16),
            jax.ShapeDtypeStruct((TAPS, 4, FILT), F32),
        ),
        in_specs=[any_space] * 5,
        out_specs=(vmem, vmem),
        scratch_shapes=scratch,
        compiler_params=pltpu.CompilerParams(
            collective_id=0, has_side_effects=True, vmem_limit_bytes=48 * 1024 * 1024
        ),
        name="layers",
    )(
        volumes[0],
        jnp.transpose(w_first),
        bias_first.reshape(1, CH),
        jnp.transpose(w_second, (1, 0, 2)),
        cotangent[0],
    )
    return pre.reshape(1, CH, 2, 4, LANES), jnp.transpose(w2g, (2, 0, 1))


def solution(mesh):
    placed = (P("samp", None, "grp", None, None), P(), P(), P(), P("samp", "grp", None, None))
    return jax.shard_map(
        on_device,
        mesh=mesh,
        in_specs=placed,
        out_specs=(P("samp", None, "grp", None, None), P(None, None, "grp")),
        check_vma=False,
    )
```

```python
import math

import jax
import jax.numpy as jnp
from jax import lax
from jax.experimental import pallas as pl
from jax.experimental.pallas import tpu as pltpu
from jax.sharding import PartitionSpec as P

MESH = pl.DeviceIdType.MESH
F32 = jnp.float32
BF16 = jnp.bfloat16

CIN = 64
CH = 128
FILT = 256
HALF = 128
LANES = 128
ZQ = 16
GRP = 32
SAMP = 8
TAPS = 27
COMBOS = [(b, e) for b in (-1, 0, 1) for e in (-1, 0, 1)]
PHASES = [(0, 0), (0, 1), (1, 0), (1, 1)]
TAP_ORDER = [t for n in range(9) for t in (18 + n, n)] + [9 + n for n in range(9)]
SLOTS = 28
ROWS_A = 64
ROWS_B = 48
ROWS = ROWS_A + ROWS_B
K_BACK = 9 * CIN
SCALE = 1.0 / math.sqrt(32768)


def lane_index(shape):
    return lax.broadcasted_iota(jnp.int32, shape, len(shape) - 1)


def y_before(x):
    return pltpu.roll(x, ZQ, 1)


def z_before(x):
    first = lane_index(x.shape) % ZQ == 0
    return jnp.where(first, pltpu.roll(x, LANES + 1 - ZQ, 1), pltpu.roll(x, 1, 1))


def row_y_after(x):
    return jnp.concatenate([x[ZQ:], x[:ZQ]], axis=0)


def row_z_after(x):
    rows = x.shape[0]
    last = lax.broadcasted_iota(jnp.int32, x.shape, 0) % ZQ == ZQ - 1
    return jnp.where(last, pltpu.roll(x, ZQ - 1, 0), pltpu.roll(x, rows - 1, 0))


def kernel(
    vol, w1t, bias, w2, cot,
    pre_out, w2_out,
    vbuf, w1tv, w1_back, w1_rest, biasv, w2v, cotv, cstg, cstage, crecv, cotf, cpart,
    perm, tn, ty, tz, tyz, hsend, hrecv, pre_s, act_own, act_part, carry, cvar, pgf,
    send_buf, recv_a, recv_b, part_a, part_b,
    lsem, vsem, halo_sem, cot_sem, cx_sem, act_sem, rs_sem, samp_sem,
):
    recv_buf = (recv_a, recv_b)
    part_buf = (part_a, part_b)
    me = lax.axis_index("grp")
    samp = lax.axis_index("samp")
    core = lax.rem(samp, 2)
    other = samp + 1 - 2 * core

    ld_cot = pltpu.make_async_copy(cot, cotv, lsem.at[0])
    ld_w1 = pltpu.make_async_copy(w1t, w1tv, lsem.at[1])
    ld_bias = pltpu.make_async_copy(bias, biasv, lsem.at[2])
    ld_w2 = pltpu.make_async_copy(w2, w2v, lsem.at[3])
    ld_vol = [pltpu.make_async_copy(vol.at[:, x], vbuf.at[x], vsem.at[x]) for x in range(4)]
    ld_cot.start()
    ld_w1.start()
    ld_bias.start()
    for x in (3, 1, 2, 0):
        ld_vol[x].start()
    ld_w2.start()

    barrier = pltpu.get_barrier_semaphore()

    def greet_grp(k, _):
        pl.semaphore_signal(
            barrier, inc=1, device_id={"grp": lax.rem(me + k, GRP)}, device_id_type=MESH
        )
        return 0

    def greet_samp(k, _):
        pl.semaphore_signal(
            barrier, inc=1, device_id={"samp": lax.rem(samp + k, SAMP)}, device_id_type=MESH
        )
        return 0

    lax.fori_loop(1, SAMP, greet_samp, 0)
    lax.fori_loop(1, GRP, greet_grp, 0)

    ld_cot.wait()
    for f in range(8):
        x = cotv[f].astype(F32)
        cstg[pl.ds(f, GRP, stride=16), :] = x
        cstg[pl.ds(8 + f, GRP, stride=16), :] = jnp.concatenate([x[1:], x[:1]], axis=0)
    cstage[...] = cstg[...].reshape(GRP, 16, LANES).astype(BF16)

    pl.semaphore_wait(barrier, GRP - 1 + SAMP - 1)

    halo = pltpu.make_async_remote_copy(
        src_ref=hsend, dst_ref=hrecv,
        send_sem=halo_sem.at[0], recv_sem=halo_sem.at[1],
        device_id={"grp": lax.rem(me + 1, GRP)}, device_id_type=MESH,
    )

    def send_cot(k, _):
        dest = lax.rem(me + k, GRP)
        pltpu.make_async_remote_copy(
            src_ref=cstage.at[dest], dst_ref=crecv.at[me],
            send_sem=cot_sem.at[0], recv_sem=cot_sem.at[1],
            device_id={"grp": dest}, device_id_type=MESH,
        ).start()
        return 0

    lax.fori_loop(1, GRP, send_cot, 0)
    crecv[me] = cstage[me]

    ld_w1.wait()
    ld_bias.wait()
    w1_back[...] = jnp.transpose(w1tv[:K_BACK, :])
    w1_rest[...] = jnp.transpose(w1tv[K_BACK:, :])
    bias_rows = jnp.transpose(jnp.broadcast_to(biasv[...], (CH, CH)))
    row = lax.broadcasted_iota(jnp.int32, (256, 256), 0)
    col = lax.broadcasted_iota(jnp.int32, (256, 256), 1)
    perm[...] = jnp.where(col == (row % 16) * 16 + row // 16, 1.0, 0.0).astype(BF16)

    def by_phase(x):
        for blk in range(4):
            rows = vbuf[x, 16 * blk : 16 * blk + 16].reshape(256, LANES)
            moved = jnp.dot(perm[...], rows, preferred_element_type=F32)
            here = slice(16 * blk, 16 * blk + 16)
            tn[x, :, here, :] = moved.reshape(16, 16, LANES).astype(BF16)
            ty[x, :, here, :] = y_before(moved[192:256]).reshape(4, 16, LANES).astype(BF16)
            ends = jnp.concatenate([moved[64 * r + 48 : 64 * r + 64] for r in range(4)], axis=0)
            ends = z_before(ends)
            tz[x, :, here, :] = ends.reshape(4, 16, LANES).astype(BF16)
            tyz[x, here, :] = y_before(ends[48:64]).astype(BF16)

    def patch(x, qy, qz, b, e):
        along_y, along_z = 2 * qy + b, 2 * qz + e
        ry, rz = along_y % 4, along_z % 4
        if along_y < 0 and along_z < 0:
            return tyz[x]
        if along_y < 0:
            return ty[x, rz]
        if along_z < 0:
            return tz[x, ry]
        return tn[x, 4 * ry + rz]

    def products(weights, planes, pair):
        columns = []
        for q in (2 * pair, 2 * pair + 1):
            qy, qz = PHASES[q]
            columns.append(
                jnp.concatenate([patch(x, qy, qz, b, e) for x in planes for b, e in COMBOS], axis=0)
            )
        return jnp.dot(
            weights[...], jnp.concatenate(columns, axis=1), preferred_element_type=F32
        )

    def activate(i, q, z):
        pre_s[i, q] = z
        act_own[i, q] = (z / (1.0 + jnp.exp(-z))).astype(BF16)

    def exchange_act(i):
        return pltpu.make_async_remote_copy(
            src_ref=act_own.at[i], dst_ref=act_part.at[i],
            send_sem=act_sem.at[0, i], recv_sem=act_sem.at[1, i],
            device_id={"samp": other}, device_id_type=MESH,
        )

    ld_vol[3].wait()
    by_phase(3)
    for pair in (0, 1):
        back = products(w1_back, (3,), pair).astype(BF16)
        hsend[2 * pair] = back[:, :LANES]
        hsend[2 * pair + 1] = back[:, LANES:]
    halo.start()

    for x in (1, 2):
        ld_vol[x].wait()
        by_phase(x)
    for pair in (0, 1):
        pre = products(w1_back, (1,), pair) + products(w1_rest, (2, 3), pair)
        for h in (0, 1):
            activate(1, 2 * pair + h, pre[:, LANES * h : LANES * (h + 1)] + bias_rows)
    act_copy = [exchange_act(0), exchange_act(1)]
    act_copy[1].start()

    ld_vol[0].wait()
    by_phase(0)
    for pair in (0, 1):
        pre = products(w1_rest, (0, 1), pair)
        for h in (0, 1):
            pre_s[0, 2 * pair + h] = pre[:, LANES * h : LANES * (h + 1)] + bias_rows

    pltpu.make_async_copy(
        crecv.at[pl.ds(0, GRP - 1)], crecv.at[pl.ds(0, GRP - 1)], cot_sem.at[1]
    ).wait()
    got = crecv[...].astype(F32)
    for p in (0, 1):
        cotf[p] = got[:, 8 * p : 8 * p + 8].reshape(FILT, LANES).astype(BF16)
    cx = pltpu.make_async_remote_copy(
        src_ref=cotf.at[:, pl.ds(pl.multiple_of(HALF * (1 - core), HALF), HALF), :], dst_ref=cpart,
        send_sem=cx_sem.at[0], recv_sem=cx_sem.at[1],
        device_id={"samp": other}, device_id_type=MESH,
    )
    cx.start()

    my_half = pl.ds(pl.multiple_of(HALF * core, HALF), HALF)

    def second_patch(i, n):
        b, e = COMBOS[n]
        phase = 2 * (b != 0) + (e != 0)
        parts = []
        for ref in (act_own, act_part):
            x = ref[i, phase]
            if b < 0 or e < 0:
                x = x.astype(F32)
                if e < 0:
                    x = z_before(x)
                if b < 0:
                    x = y_before(x)
                x = x.astype(BF16)
            parts.append(x)
        return jnp.concatenate(parts, axis=1)

    contract = (((1,), (1,)), ((), ()))

    def pack(group, taps):
        low = lax.broadcasted_iota(jnp.int32, (16, 8, LANES), 1) < 4
        t = [x.reshape(16, 8, LANES) for x in taps]
        turned = [pltpu.roll(x, 4, 1) for x in t]
        even = [jnp.where(low, t[j], turned[j + 1]) for j in (0, 2)]
        odd = [jnp.where(low, turned[j], t[j + 1]) for j in (0, 2)]
        rows = slice(16 * group, 16 * group + 16)
        send_buf[:, 0, rows, :] = jnp.concatenate(even, axis=1).astype(BF16)
        send_buf[:, 1, rows, :] = jnp.concatenate(odd, axis=1).astype(BF16)

    def send_chunk(which):
        rows = pl.ds(0, ROWS_A) if which == 0 else pl.ds(ROWS_A, ROWS_B)

        def body(k, _):
            dest = lax.rem(me + k, GRP)
            pltpu.make_async_remote_copy(
                src_ref=send_buf.at[lax.div(dest, 2), lax.rem(dest, 2), rows],
                dst_ref=recv_buf[which].at[k - 1],
                send_sem=rs_sem.at[0, which], recv_sem=rs_sem.at[1, which],
                device_id={"grp": dest}, device_id_type=MESH,
            ).start()
            return 0

        lax.fori_loop(1, GRP, body, 0)

    def cot_rhs(p):
        return jnp.concatenate([cotf[p, my_half, :], cpart[p]], axis=1)

    act_copy[1].wait_recv()
    cx.wait_recv()
    rhs_both = jnp.concatenate([cot_rhs(0), cot_rhs(1)], axis=0)
    held = []
    for n in range(9):
        d = lax.dot_general(second_patch(1, n), rhs_both, contract, preferred_element_type=F32)
        held += [d[:, :LANES], d[:, LANES:]]
        if len(held) == 4:
            pack(n // 2, held)
            held = []
    carry[0] = held[0]
    carry[1] = held[1]
    send_chunk(0)

    halo.wait_recv()
    for q in range(4):
        activate(0, q, pre_s[0, q] + hrecv[q].astype(F32))
    act_copy[0].start()

    for p in (0, 1):
        turned = jnp.transpose(cotf[p].astype(F32))
        cvar[p, 0] = turned.astype(BF16)
        cvar[p, 2] = row_y_after(turned).astype(BF16)
        after = row_z_after(turned)
        cvar[p, 1] = after.astype(BF16)
        cvar[p, 3] = row_y_after(after).astype(BF16)

    act_copy[0].wait_recv()
    rhs_one = cot_rhs(0)
    held = [carry[0], carry[1]]
    group = 4
    for n in range(9):
        held.append(
            lax.dot_general(second_patch(0, n), rhs_one, contract, preferred_element_type=F32)
        )
        if len(held) == 4:
            pack(group, held)
            group += 1
            held = []
    pack(group, held + [jnp.zeros((CH, LANES), F32)] * (4 - len(held)))
    send_chunk(1)

    ld_w2.wait()
    for i in (0, 1):
        for q, (qy, qz) in enumerate(PHASES):
            left, right = [], []
            for a, p in ((0, 0),) if i == 0 else ((1, 0), (-1, 1)):
                for b, sy in ((0, 0),) if qy == 0 else ((1, 0), (-1, 1)):
                    for e, sz in ((0, 0),) if qz == 0 else ((1, 0), (-1, 1)):
                        left.append(cvar[p, 2 * sy + sz])
                        right.append(w2v[9 * (a + 1) + 3 * (b + 1) + e + 1])
            grad = jnp.dot(
                jnp.concatenate(left, axis=1),
                jnp.concatenate(right, axis=0),
                preferred_element_type=F32,
            )
            grad = jnp.transpose(grad.astype(BF16).astype(F32))
            z = pre_s[i, q]
            g = 1.0 / (1.0 + jnp.exp(-z))
            pgf[pl.ds(4 * i + q, CH, stride=8), :] = grad * (g * (1.0 + z * (1.0 - g)))
    pre_out[...] = pgf[...].reshape(CH, 8, LANES).astype(BF16)

    mine = send_buf.at[lax.div(me, 2), lax.rem(me, 2)]
    chunk_rows = (pl.ds(0, ROWS_A), pl.ds(ROWS_A, ROWS_B))
    for which in (0, 1):
        received, parts = recv_buf[which], part_buf[which]
        pltpu.make_async_copy(received, received, rs_sem.at[1, which]).wait()
        parts[samp] = lax.fori_loop(
            0,
            GRP - 1,
            lambda j, acc, received=received: acc + received[j].astype(F32),
            mine[chunk_rows[which], :].astype(F32),
        ).astype(BF16)

        def send_part(k, _, parts=parts, which=which):
            pltpu.make_async_remote_copy(
                src_ref=parts.at[samp], dst_ref=parts.at[samp],
                send_sem=samp_sem.at[0, which], recv_sem=samp_sem.at[1, which],
                device_id={"samp": lax.rem(samp + k, SAMP)}, device_id_type=MESH,
            ).start()
            return 0

        lax.fori_loop(1, SAMP, send_part, 0)

    for which in (0, 1):
        parts = part_buf[which]
        seven = parts.at[pl.ds(0, SAMP - 1)]
        pltpu.make_async_copy(seven, seven, samp_sem.at[1, which]).wait()
        for h in (0, 1):
            total = sum(parts[h + 2 * j].astype(F32) for j in range(SAMP // 2)) * SCALE
            first = 0 if which == 0 else ROWS_A // 4
            for slot in range(total.shape[0] // 4):
                if first + slot < TAPS:
                    w2_out[TAP_ORDER[first + slot], :, LANES * h : LANES * (h + 1)] = total[
                        4 * slot : 4 * slot + 4
                    ]

    halo.wait_send()
    pltpu.make_async_copy(
        cstage.at[pl.ds(0, GRP - 1)], cstage.at[pl.ds(0, GRP - 1)], cot_sem.at[0]
    ).wait()
    cx.wait_send()
    for c in act_copy:
        c.wait_send()
    for which in (0, 1):
        pltpu.make_async_copy(recv_buf[which], recv_buf[which], rs_sem.at[0, which]).wait()
        seven = part_buf[which].at[pl.ds(0, SAMP - 1)]
        pltpu.make_async_copy(seven, seven, samp_sem.at[0, which]).wait()


def on_device(volumes, w_first, bias_first, w_second, cotangent):
    any_space = pl.BlockSpec(memory_space=pltpu.HBM)
    vmem = pl.BlockSpec(memory_space=pltpu.VMEM)
    dma = pltpu.SemaphoreType.DMA
    scratch = [
        pltpu.VMEM((4, CIN, 16, LANES), BF16),
        pltpu.VMEM((TAPS * CIN, CH), BF16),
        pltpu.VMEM((CH, K_BACK), BF16),
        pltpu.VMEM((CH, TAPS * CIN - K_BACK), BF16),
        pltpu.VMEM((1, CH), F32),
        pltpu.VMEM((TAPS, FILT, CH), BF16),
        pltpu.VMEM((8, GRP, LANES), BF16),
        pltpu.VMEM((GRP * 16, LANES), F32),
        pltpu.VMEM((GRP, 16, LANES), BF16),
        pltpu.VMEM((GRP, 16, LANES), BF16),
        pltpu.VMEM((2, FILT, LANES), BF16),
        pltpu.VMEM((2, HALF, LANES), BF16),
        pltpu.VMEM((256, 256), BF16),
        pltpu.VMEM((4, 16, CIN, LANES), BF16),
        pltpu.VMEM((4, 4, CIN, LANES), BF16),
        pltpu.VMEM((4, 4, CIN, LANES), BF16),
        pltpu.VMEM((4, CIN, LANES), BF16),
        pltpu.VMEM((4, CH, LANES), BF16),
        pltpu.VMEM((4, CH, LANES), BF16),
        pltpu.VMEM((2, 4, CH, LANES), F32),
        pltpu.VMEM((2, 4, CH, LANES), BF16),
        pltpu.VMEM((2, 4, CH, LANES), BF16),
        pltpu.VMEM((2, CH, LANES), F32),
        pltpu.VMEM((2, 4, LANES, FILT), BF16),
        pltpu.VMEM((CH * 8, LANES), F32),
        pltpu.VMEM((GRP // 2, 2, ROWS, LANES), BF16),
        pltpu.VMEM((GRP - 1, ROWS_A, LANES), BF16),
        pltpu.VMEM((GRP - 1, ROWS_B, LANES), BF16),
        pltpu.VMEM((SAMP, ROWS_A, LANES), BF16),
        pltpu.VMEM((SAMP, ROWS_B, LANES), BF16),
        dma((4,)),
        dma((4,)),
        dma((2,)),
        dma((2,)),
        dma((2,)),
        dma((2, 2)),
        dma((2, 2)),
        dma((2, 2)),
    ]

    pre, w2g = pl.pallas_call(
        kernel,
        out_shape=(
            jax.ShapeDtypeStruct((CH, 8, LANES), BF16),
            jax.ShapeDtypeStruct((TAPS, 4, FILT), F32),
        ),
        in_specs=[any_space] * 5,
        out_specs=(vmem, vmem),
        scratch_shapes=scratch,
        compiler_params=pltpu.CompilerParams(
            collective_id=0, has_side_effects=True, vmem_limit_bytes=60 * 1024 * 1024
        ),
        name="layers",
    )(
        volumes[0],
        jnp.transpose(w_first),
        bias_first.reshape(1, CH),
        jnp.transpose(w_second, (1, 0, 2)),
        cotangent[0],
    )
    return pre.reshape(1, CH, 2, 4, LANES), jnp.transpose(w2g, (2, 0, 1))


def solution(mesh):
    placed = (P("samp", None, "grp", None, None), P(), P(), P(), P("samp", "grp", None, None))
    return jax.shard_map(
        on_device,
        mesh=mesh,
        in_specs=placed,
        out_specs=(P("samp", None, "grp", None, None), P(None, None, "grp")),
        check_vma=False,
    )
```

```python
import math

import jax
import jax.numpy as jnp
from jax import lax
from jax.experimental import pallas as pl
from jax.experimental.pallas import tpu as pltpu
from jax.sharding import PartitionSpec as P

MESH = pl.DeviceIdType.MESH
F32 = jnp.float32
BF16 = jnp.bfloat16

CIN = 64
CH = 128
FILT = 256
LANES = 128
ZQ = 16
GRP = 32
SAMP = 8
TAPS = 27
COMBOS = [(b, e) for b in (-1, 0, 1) for e in (-1, 0, 1)]
PHASES = [(0, 0), (0, 1), (1, 0), (1, 1)]
QUARTER = 32
ROWS = 32
CHUNK_TAPS = (((0, 8), (18, 8)), ((8, 10), (26, 1)))
CHUNK_HALF = (16, 12)
OUT_ROWS = 112
K_BACK = 9 * CIN
SCALE = 1.0 / math.sqrt(32768)


def lane_index(shape):
    return lax.broadcasted_iota(jnp.int32, shape, len(shape) - 1)


def y_before(x):
    return pltpu.roll(x, ZQ, 1)


def z_before(x):
    first = lane_index(x.shape) % ZQ == 0
    return jnp.where(first, pltpu.roll(x, LANES + 1 - ZQ, 1), pltpu.roll(x, 1, 1))


def row_y_after(x):
    return jnp.concatenate([x[ZQ:], x[:ZQ]], axis=0)


def row_z_after(x):
    rows = x.shape[0]
    last = lax.broadcasted_iota(jnp.int32, x.shape, 0) % ZQ == ZQ - 1
    return jnp.where(last, pltpu.roll(x, ZQ - 1, 0), pltpu.roll(x, rows - 1, 0))


def kernel(
    vol, w1t, bias, w2, cot,
    pre_out, w2_out,
    vbuf, w1tv, w1_back, w1_rest, biasv, w2v, cotv, cot_32, cstg, cstage, crecv, cots,
    perm, tn, ty, tz, tyz, hsend, hrecv, pre_s, act_32, act_own, act_in, cvar, pgf,
    stage, send_buf, recv_a, recv_b, part_a, part_b, fin,
    lsem, vsem, halo_sem, cot_sem, cx_sem, act_sem, rs_sem, samp_sem,
):
    recv_buf = (recv_a, recv_b)
    part_buf = (part_a, part_b)
    me = lax.axis_index("grp")
    samp = lax.axis_index("samp")
    core = lax.rem(samp, 2)
    other = samp + 1 - 2 * core
    odd = lax.rem(me, 2)
    quarter = 2 * core + odd

    ld_cot = pltpu.make_async_copy(cot, cotv, lsem.at[0])
    ld_w1 = pltpu.make_async_copy(w1t, w1tv, lsem.at[1])
    ld_bias = pltpu.make_async_copy(bias, biasv, lsem.at[2])
    ld_w2 = pltpu.make_async_copy(w2, w2v, lsem.at[3])
    ld_vol = [pltpu.make_async_copy(vol.at[:, x], vbuf.at[x], vsem.at[x]) for x in range(4)]
    ld_cot.start()
    ld_w1.start()
    ld_bias.start()
    for x in (3, 1, 2, 0):
        ld_vol[x].start()
    ld_w2.start()

    barrier = pltpu.get_barrier_semaphore()

    def greet_grp(k, _):
        pl.semaphore_signal(
            barrier, inc=1, device_id={"grp": lax.rem(me + k, GRP)}, device_id_type=MESH
        )
        return 0

    def greet_samp(k, _):
        pl.semaphore_signal(
            barrier, inc=1, device_id={"samp": lax.rem(samp + k, SAMP)}, device_id_type=MESH
        )
        return 0

    lax.fori_loop(1, SAMP, greet_samp, 0)
    lax.fori_loop(1, GRP, greet_grp, 0)
    pl.semaphore_signal(
        barrier, inc=1, device_id={"samp": other, "grp": me + 1 - 2 * odd}, device_id_type=MESH
    )

    ld_cot.wait()
    for f in range(8):
        x = cotv[f].astype(F32)
        cot_32[40 * f : 40 * f + GRP, :] = x
        cot_32[40 * f + GRP : 40 * f + 40, :] = x[:8]
    for f in range(8):
        for p in range(4):
            cstg[pl.ds(8 * p + f, GRP // 2, stride=32), :] = cot_32[
                pl.ds(40 * f + p, GRP // 2, stride=2), :
            ]
    cstage[...] = cstg[...].reshape(GRP // 2, 32, LANES).astype(BF16)

    ld_w1.wait()
    ld_bias.wait()
    w1_back[...] = jnp.transpose(w1tv[:K_BACK, :])
    w1_rest[...] = jnp.transpose(w1tv[K_BACK:, :])
    bias_rows = jnp.transpose(jnp.broadcast_to(biasv[...], (CH, CH)))
    row = lax.broadcasted_iota(jnp.int32, (256, 256), 0)
    col = lax.broadcasted_iota(jnp.int32, (256, 256), 1)
    perm[...] = jnp.where(col == (row % 16) * 16 + row // 16, 1.0, 0.0).astype(BF16)

    def by_phase(x):
        for blk in range(4):
            rows = vbuf[x, 16 * blk : 16 * blk + 16].reshape(256, LANES)
            moved = jnp.dot(perm[...], rows, preferred_element_type=F32)
            here = slice(16 * blk, 16 * blk + 16)
            tn[x, :, here, :] = moved.reshape(16, 16, LANES).astype(BF16)
            ty[x, :, here, :] = y_before(moved[192:256]).reshape(4, 16, LANES).astype(BF16)
            ends = jnp.concatenate([moved[64 * r + 48 : 64 * r + 64] for r in range(4)], axis=0)
            ends = z_before(ends)
            tz[x, :, here, :] = ends.reshape(4, 16, LANES).astype(BF16)
            tyz[x, here, :] = y_before(ends[48:64]).astype(BF16)

    def patch(x, qy, qz, b, e):
        along_y, along_z = 2 * qy + b, 2 * qz + e
        ry, rz = along_y % 4, along_z % 4
        if along_y < 0 and along_z < 0:
            return tyz[x]
        if along_y < 0:
            return ty[x, rz]
        if along_z < 0:
            return tz[x, ry]
        return tn[x, 4 * ry + rz]

    def products(weights, planes, pair):
        columns = []
        for q in (2 * pair, 2 * pair + 1):
            qy, qz = PHASES[q]
            columns.append(
                jnp.concatenate([patch(x, qy, qz, b, e) for x in planes for b, e in COMBOS], axis=0)
            )
        return jnp.dot(
            weights[...], jnp.concatenate(columns, axis=1), preferred_element_type=F32
        )

    def activate(i, q, z):
        pre_s[i, q] = z
        act_32[...] = z / (1.0 + jnp.exp(-z))
        for r in range(4):
            act_own[i, r, q] = act_32[pl.ds(r, QUARTER, stride=4), :].astype(BF16)

    def send_act(i):
        def body(k, _):
            to = lax.rem(quarter + k, 4)
            pltpu.make_async_remote_copy(
                src_ref=act_own.at[i, to], dst_ref=act_in.at[i, quarter],
                send_sem=act_sem.at[0, i], recv_sem=act_sem.at[1, i],
                device_id={
                    "samp": samp - core + lax.div(to, 2),
                    "grp": me - odd + lax.rem(to, 2),
                },
                device_id_type=MESH,
            ).start()
            return 0

        lax.fori_loop(1, 4, body, 0)
        act_in[i, quarter] = act_own[i, quarter]

    def wait_act(i, end):
        three = act_in.at[i, pl.ds(0, 3)]
        pltpu.make_async_copy(three, three, act_sem.at[end, i]).wait()

    ld_vol[3].wait()
    by_phase(3)
    for pair in (0, 1):
        back = products(w1_back, (3,), pair).astype(BF16)
        hsend[2 * pair] = back[:, :LANES]
        hsend[2 * pair + 1] = back[:, LANES:]
    stage[...] = jnp.zeros_like(stage)

    pl.semaphore_wait(barrier, GRP - 1 + SAMP - 1 + 1)

    halo = pltpu.make_async_remote_copy(
        src_ref=hsend, dst_ref=hrecv,
        send_sem=halo_sem.at[0], recv_sem=halo_sem.at[1],
        device_id={"grp": lax.rem(me + 1, GRP)}, device_id_type=MESH,
    )

    def send_cot(k, _):
        dest = lax.rem(me + k, GRP)
        pltpu.make_async_remote_copy(
            src_ref=cstage.at[lax.div(dest, 2)], dst_ref=crecv.at[me],
            send_sem=cot_sem.at[0], recv_sem=cot_sem.at[1],
            device_id={"grp": dest}, device_id_type=MESH,
        ).start()
        return 0

    lax.fori_loop(1, GRP, send_cot, 0)
    crecv[me] = cstage[lax.div(me, 2)]
    halo.start()

    for x in (1, 2):
        ld_vol[x].wait()
        by_phase(x)
    for pair in (0, 1):
        pre = products(w1_back, (1,), pair) + products(w1_rest, (2, 3), pair)
        for h in (0, 1):
            activate(1, 2 * pair + h, pre[:, LANES * h : LANES * (h + 1)] + bias_rows)
    send_act(1)

    ld_vol[0].wait()
    by_phase(0)
    for pair in (0, 1):
        pre = products(w1_rest, (0, 1), pair)
        for h in (0, 1):
            pre_s[0, 2 * pair + h] = pre[:, LANES * h : LANES * (h + 1)] + bias_rows

    pltpu.make_async_copy(
        crecv.at[pl.ds(0, GRP - 1)], crecv.at[pl.ds(0, GRP - 1)], cot_sem.at[1]
    ).wait()
    got = crecv[...].astype(F32)
    for p in range(3):
        cots[core, p] = got[:, 8 * p : 8 * p + 8].reshape(FILT, LANES).astype(BF16)
    cx = pltpu.make_async_remote_copy(
        src_ref=cots.at[core], dst_ref=cots.at[core],
        send_sem=cx_sem.at[0], recv_sem=cx_sem.at[1],
        device_id={"samp": other}, device_id_type=MESH,
    )
    cx.start()

    def second_patch(i, n):
        b, e = COMBOS[n]
        x = act_in[i, :, 2 * (b != 0) + (e != 0)].reshape(4 * QUARTER, LANES)
        if b < 0 or e < 0:
            x = x.astype(F32)
            if e < 0:
                x = z_before(x)
            if b < 0:
                x = y_before(x)
            x = x.astype(BF16)
        return jnp.concatenate([x[QUARTER * j : QUARTER * (j + 1)] for j in range(4)], axis=1)

    def filter_products(i, steps):
        left = jnp.concatenate([second_patch(i, n) for n in range(9)], axis=0)
        right = [
            jnp.concatenate([cots[j // 2, j % 2 + step] for j in range(4)], axis=1)
            for step in steps
        ]
        return lax.dot_general(
            left,
            jnp.concatenate(right, axis=0),
            (((1,), (1,)), ((), ())),
            preferred_element_type=F32,
        )

    def place(tap, rows):
        for which in (0, 1):
            at = 0
            for first, count in CHUNK_TAPS[which]:
                if first <= tap < first + count:
                    for h in (0, 1):
                        row = ROWS * which + CHUNK_HALF[which] * h + at + tap - first
                        stage[pl.ds(row, GRP, stride=2 * ROWS), :] = rows[
                            :, LANES * h : LANES * (h + 1)
                        ]
                at += count

    def send_chunk(which):
        staged = stage[...].reshape(GRP, 2 * ROWS, LANES)[:, ROWS * which : ROWS * (which + 1)]
        send_buf[which] = staged.astype(BF16)
        recv_buf[which][me] = send_buf[which, me]

        def body(k, _):
            dest = lax.rem(me + k, GRP)
            pltpu.make_async_remote_copy(
                src_ref=send_buf.at[which, dest], dst_ref=recv_buf[which].at[me],
                send_sem=rs_sem.at[0, which], recv_sem=rs_sem.at[1, which],
                device_id={"grp": dest}, device_id_type=MESH,
            ).start()
            return 0

        lax.fori_loop(1, GRP, body, 0)

    wait_act(1, 1)
    cx.wait_recv()
    grads = filter_products(1, (0, 1))
    for n in range(9):
        rows = grads[QUARTER * n : QUARTER * (n + 1)]
        place(18 + n, rows[:, :FILT])
        place(n, rows[:, FILT:])
    send_chunk(0)

    halo.wait_recv()
    for q in range(4):
        activate(0, q, pre_s[0, q] + hrecv[q].astype(F32))
    send_act(0)

    for p in (0, 1):
        turned = jnp.transpose(cots[core, odd + p].astype(F32))
        cvar[p, 0] = turned.astype(BF16)
        cvar[p, 2] = row_y_after(turned).astype(BF16)
        after = row_z_after(turned)
        cvar[p, 1] = after.astype(BF16)
        cvar[p, 3] = row_y_after(after).astype(BF16)

    wait_act(0, 1)
    grads = filter_products(0, (0,))
    for n in range(9):
        place(9 + n, grads[QUARTER * n : QUARTER * (n + 1)])
    send_chunk(1)

    ld_w2.wait()
    for i in (0, 1):
        for q, (qy, qz) in enumerate(PHASES):
            left, right = [], []
            for a, p in ((0, 0),) if i == 0 else ((1, 0), (-1, 1)):
                for b, sy in ((0, 0),) if qy == 0 else ((1, 0), (-1, 1)):
                    for e, sz in ((0, 0),) if qz == 0 else ((1, 0), (-1, 1)):
                        left.append(cvar[p, 2 * sy + sz])
                        right.append(w2v[9 * (a + 1) + 3 * (b + 1) + e + 1])
            grad = jnp.dot(
                jnp.concatenate(left, axis=1),
                jnp.concatenate(right, axis=0),
                preferred_element_type=F32,
            )
            grad = jnp.transpose(grad.astype(BF16).astype(F32))
            z = pre_s[i, q]
            g = 1.0 / (1.0 + jnp.exp(-z))
            pgf[pl.ds(4 * i + q, CH, stride=8), :] = grad * (g * (1.0 + z * (1.0 - g)))
    pre_out[...] = pgf[...].reshape(CH, 8, LANES).astype(BF16)

    most = pl.ds(0, GRP - 1)
    for which in (0, 1):
        received, parts = recv_buf[which], part_buf[which]
        pltpu.make_async_copy(received.at[most], received.at[most], rs_sem.at[1, which]).wait()
        total = lax.fori_loop(
            0,
            GRP // 2,
            lambda j, acc, received=received: acc + received[pl.ds(2 * j, 2)].astype(F32),
            jnp.zeros((2, ROWS, LANES), F32),
        )
        used = 2 * CHUNK_HALF[which]
        parts[samp] = total[:, :used].reshape(2 * used, LANES).astype(BF16)

        def send_part(k, _, parts=parts, which=which):
            pltpu.make_async_remote_copy(
                src_ref=parts.at[samp], dst_ref=parts.at[samp],
                send_sem=samp_sem.at[0, which], recv_sem=samp_sem.at[1, which],
                device_id={"samp": lax.rem(samp + k, SAMP)}, device_id_type=MESH,
            ).start()
            return 0

        lax.fori_loop(1, SAMP, send_part, 0)

    for which in (0, 1):
        parts, half = part_buf[which], CHUNK_HALF[which]
        seven = parts.at[pl.ds(0, SAMP - 1)]
        pltpu.make_async_copy(seven, seven, samp_sem.at[1, which]).wait()
        for k in (0, 1):
            total = sum(parts[k + 2 * j].astype(F32) for j in range(SAMP // 2)) * SCALE
            for parity in (0, 1):
                for h in (0, 1):
                    at = half * (2 * parity + h)
                    for first, count in CHUNK_TAPS[which]:
                        row = OUT_ROWS * h + 4 * first + 2 * k + parity
                        fin[pl.ds(row, count, stride=4), :] = total[at : at + count]
                        at += count
    for tap in range(TAPS):
        for h in (0, 1):
            row = OUT_ROWS * h + 4 * tap
            w2_out[tap, :, LANES * h : LANES * (h + 1)] = fin[row : row + 4, :]

    halo.wait_send()
    pltpu.make_async_copy(
        crecv.at[most], crecv.at[most], cot_sem.at[0]
    ).wait()
    cx.wait_send()
    wait_act(0, 0)
    wait_act(1, 0)
    for which in (0, 1):
        sent = recv_buf[which].at[most]
        pltpu.make_async_copy(sent, sent, rs_sem.at[0, which]).wait()
        seven = part_buf[which].at[pl.ds(0, SAMP - 1)]
        pltpu.make_async_copy(seven, seven, samp_sem.at[0, which]).wait()


def on_device(volumes, w_first, bias_first, w_second, cotangent):
    any_space = pl.BlockSpec(memory_space=pltpu.HBM)
    vmem = pl.BlockSpec(memory_space=pltpu.VMEM)
    dma = pltpu.SemaphoreType.DMA
    scratch = [
        pltpu.VMEM((4, CIN, 16, LANES), BF16),
        pltpu.VMEM((TAPS * CIN, CH), BF16),
        pltpu.VMEM((CH, K_BACK), BF16),
        pltpu.VMEM((CH, TAPS * CIN - K_BACK), BF16),
        pltpu.VMEM((1, CH), F32),
        pltpu.VMEM((TAPS, FILT, CH), BF16),
        pltpu.VMEM((8, GRP, LANES), BF16),
        pltpu.VMEM((8 * 40, LANES), F32),
        pltpu.VMEM((GRP // 2 * 32, LANES), F32),
        pltpu.VMEM((GRP // 2, 32, LANES), BF16),
        pltpu.VMEM((GRP, 32, LANES), BF16),
        pltpu.VMEM((2, 3, FILT, LANES), BF16),
        pltpu.VMEM((256, 256), BF16),
        pltpu.VMEM((4, 16, CIN, LANES), BF16),
        pltpu.VMEM((4, 4, CIN, LANES), BF16),
        pltpu.VMEM((4, 4, CIN, LANES), BF16),
        pltpu.VMEM((4, CIN, LANES), BF16),
        pltpu.VMEM((4, CH, LANES), BF16),
        pltpu.VMEM((4, CH, LANES), BF16),
        pltpu.VMEM((2, 4, CH, LANES), F32),
        pltpu.VMEM((CH, LANES), F32),
        pltpu.VMEM((2, 4, 4, QUARTER, LANES), BF16),
        pltpu.VMEM((2, 4, 4, QUARTER, LANES), BF16),
        pltpu.VMEM((2, 4, LANES, FILT), BF16),
        pltpu.VMEM((CH * 8, LANES), F32),
        pltpu.VMEM((GRP * 2 * ROWS, LANES), F32),
        pltpu.VMEM((2, GRP, ROWS, LANES), BF16),
        pltpu.VMEM((GRP, ROWS, LANES), BF16),
        pltpu.VMEM((GRP, ROWS, LANES), BF16),
        pltpu.VMEM((SAMP, 4 * CHUNK_HALF[0], LANES), BF16),
        pltpu.VMEM((SAMP, 4 * CHUNK_HALF[1], LANES), BF16),
        pltpu.VMEM((2 * OUT_ROWS, LANES), F32),
        dma((4,)),
        dma((4,)),
        dma((2,)),
        dma((2,)),
        dma((2,)),
        dma((2, 2)),
        dma((2, 2)),
        dma((2, 2)),
    ]

    pre, w2g = pl.pallas_call(
        kernel,
        out_shape=(
            jax.ShapeDtypeStruct((CH, 8, LANES), BF16),
            jax.ShapeDtypeStruct((TAPS, 4, FILT), F32),
        ),
        in_specs=[any_space] * 5,
        out_specs=(vmem, vmem),
        scratch_shapes=scratch,
        compiler_params=pltpu.CompilerParams(
            collective_id=0, has_side_effects=True, vmem_limit_bytes=60 * 1024 * 1024
        ),
        name="layers",
    )(
        volumes[0],
        jnp.transpose(w_first),
        bias_first.reshape(1, CH),
        jnp.transpose(w_second, (1, 0, 2)),
        cotangent[0],
    )
    return pre.reshape(1, CH, 2, 4, LANES), jnp.transpose(w2g, (2, 0, 1))


def solution(mesh):
    placed = (P("samp", None, "grp", None, None), P(), P(), P(), P("samp", "grp", None, None))
    return jax.shard_map(
        on_device,
        mesh=mesh,
        in_specs=placed,
        out_specs=(P("samp", None, "grp", None, None), P(None, None, "grp")),
        check_vma=False,
    )
```

```python
import math

import jax
import jax.numpy as jnp
from jax import lax
from jax.experimental import pallas as pl
from jax.experimental.pallas import tpu as pltpu
from jax.sharding import PartitionSpec as P

MESH = pl.DeviceIdType.MESH
F32 = jnp.float32
BF16 = jnp.bfloat16

CIN = 64
CH = 128
FILT = 256
HALF = 128
LANES = 128
ZQ = 16
GRP = 32
SAMP = 8
TAPS = 27
COMBOS = [(b, e) for b in (-1, 0, 1) for e in (-1, 0, 1)]
PHASES = [(0, 0), (0, 1), (1, 0), (1, 1)]
TAP_ORDER = [t for n in range(9) for t in (18 + n, n)] + [9 + n for n in range(9)]
CHUNK_ROWS = (64, 32, 16)
CHUNK_START = (0, 64, 96)
CHUNKS = range(len(CHUNK_ROWS))
ROWS = sum(CHUNK_ROWS)
K_BACK = 9 * CIN
SCALE = 1.0 / math.sqrt(32768)


def lane_index(shape):
    return lax.broadcasted_iota(jnp.int32, shape, len(shape) - 1)


def y_before(x):
    return pltpu.roll(x, ZQ, 1)


def z_before(x):
    first = lane_index(x.shape) % ZQ == 0
    return jnp.where(first, pltpu.roll(x, LANES + 1 - ZQ, 1), pltpu.roll(x, 1, 1))


def row_y_after(x):
    return jnp.concatenate([x[ZQ:], x[:ZQ]], axis=0)


def row_z_after(x):
    rows = x.shape[0]
    last = lax.broadcasted_iota(jnp.int32, x.shape, 0) % ZQ == ZQ - 1
    return jnp.where(last, pltpu.roll(x, ZQ - 1, 0), pltpu.roll(x, rows - 1, 0))


def kernel(
    vol, w1t, bias, w2, cot,
    pre_out, w2_out,
    vbuf, w1tv, w1_back, w1_rest, biasv, w2v, cotv, cstg, cstage, crecv, cotf, cpart,
    perm, tn, ty, tz, tyz, hsend, hrecv, pre_s, act_own, act_part, carry, cvar, pgf, pre_v,
    send_buf, recv_a, recv_b, recv_c, part_a, part_b, part_c,
    lsem, vsem, halo_sem, cot_sem, cx_sem, act_sem, rs_sem, samp_sem,
):
    recv_buf = (recv_a, recv_b, recv_c)
    part_buf = (part_a, part_b, part_c)
    me = lax.axis_index("grp")
    samp = lax.axis_index("samp")
    core = lax.rem(samp, 2)
    other = samp + 1 - 2 * core

    def peer(j):
        def step(v):
            return 2 + lax.div(v * (7 - v), 2)

        z = lax.rem(lax.div(me, 16) + 1 + lax.div(j, 16), 2)
        x = lax.rem(lax.rem(lax.div(me, 4), 4) + step(lax.rem(lax.div(j, 4), 4)), 4)
        y = lax.rem(lax.rem(me, 4) + step(lax.rem(j, 4)), 4)
        return 16 * z + 4 * x + y

    def ring_peer(j):
        return lax.rem(me + 1 + j, GRP)

    def samp_peer(j):
        return lax.rem(samp + 4 + j + lax.div(j, 4), SAMP)

    ld_cot = pltpu.make_async_copy(cot, cotv, lsem.at[0])
    ld_w1 = pltpu.make_async_copy(w1t, w1tv, lsem.at[1])
    ld_bias = pltpu.make_async_copy(bias, biasv, lsem.at[2])
    ld_w2 = pltpu.make_async_copy(w2, w2v, lsem.at[3])
    ld_vol = [pltpu.make_async_copy(vol.at[:, x], vbuf.at[x], vsem.at[x]) for x in range(4)]
    ld_cot.start()
    ld_w1.start()
    ld_bias.start()
    for x in (3, 1, 2, 0):
        ld_vol[x].start()
    ld_w2.start()

    barrier = pltpu.get_barrier_semaphore()

    def greet_grp(j, _):
        pl.semaphore_signal(barrier, inc=1, device_id={"grp": peer(j)}, device_id_type=MESH)
        return 0

    def greet_samp(j, _):
        pl.semaphore_signal(barrier, inc=1, device_id={"samp": samp_peer(j)}, device_id_type=MESH)
        return 0

    lax.fori_loop(0, SAMP - 1, greet_samp, 0)
    lax.fori_loop(0, GRP - 1, greet_grp, 0)

    ld_cot.wait()
    for f in range(8):
        x = cotv[f].astype(F32)
        cstg[pl.ds(f, GRP, stride=16), :] = x
        cstg[pl.ds(8 + f, GRP, stride=16), :] = jnp.concatenate([x[1:], x[:1]], axis=0)
    cstage[...] = cstg[...].reshape(GRP, 16, LANES).astype(BF16)

    ld_w1.wait()
    ld_bias.wait()
    w1_back[...] = jnp.transpose(w1tv[:K_BACK, :])
    w1_rest[...] = jnp.transpose(w1tv[K_BACK:, :])
    bias_rows = jnp.transpose(jnp.broadcast_to(biasv[...], (CH, CH)))
    row = lax.broadcasted_iota(jnp.int32, (256, 256), 0)
    col = lax.broadcasted_iota(jnp.int32, (256, 256), 1)
    perm[...] = jnp.where(col == (row % 16) * 16 + row // 16, 1.0, 0.0).astype(BF16)

    def by_phase(x):
        for blk in range(4):
            rows = vbuf[x, 16 * blk : 16 * blk + 16].reshape(256, LANES)
            moved = jnp.dot(perm[...], rows, preferred_element_type=F32)
            here = slice(16 * blk, 16 * blk + 16)
            tn[x, :, here, :] = moved.reshape(16, 16, LANES).astype(BF16)
            ty[x, :, here, :] = y_before(moved[192:256]).reshape(4, 16, LANES).astype(BF16)
            ends = jnp.concatenate([moved[64 * r + 48 : 64 * r + 64] for r in range(4)], axis=0)
            ends = z_before(ends)
            tz[x, :, here, :] = ends.reshape(4, 16, LANES).astype(BF16)
            tyz[x, here, :] = y_before(ends[48:64]).astype(BF16)

    def patch(x, qy, qz, b, e):
        along_y, along_z = 2 * qy + b, 2 * qz + e
        ry, rz = along_y % 4, along_z % 4
        if along_y < 0 and along_z < 0:
            return tyz[x]
        if along_y < 0:
            return ty[x, rz]
        if along_z < 0:
            return tz[x, ry]
        return tn[x, 4 * ry + rz]

    def products(weights, planes, pair):
        columns = []
        for q in (2 * pair, 2 * pair + 1):
            qy, qz = PHASES[q]
            columns.append(
                jnp.concatenate([patch(x, qy, qz, b, e) for x in planes for b, e in COMBOS], axis=0)
            )
        return jnp.dot(
            weights[...], jnp.concatenate(columns, axis=1), preferred_element_type=F32
        )

    def activate(i, q, z):
        pre_s[i, q] = z
        act_own[i, q] = (z / (1.0 + jnp.exp(-z))).astype(BF16)

    def exchange_act(i):
        return pltpu.make_async_remote_copy(
            src_ref=act_own.at[i], dst_ref=act_part.at[i],
            send_sem=act_sem.at[0, i], recv_sem=act_sem.at[1, i],
            device_id={"samp": other}, device_id_type=MESH,
        )

    ld_vol[3].wait()
    by_phase(3)
    for pair in (0, 1):
        back = products(w1_back, (3,), pair).astype(BF16)
        hsend[2 * pair] = back[:, :LANES]
        hsend[2 * pair + 1] = back[:, LANES:]
    pl.semaphore_wait(barrier, GRP - 1 + SAMP - 1)

    halo = pltpu.make_async_remote_copy(
        src_ref=hsend, dst_ref=hrecv,
        send_sem=halo_sem.at[0], recv_sem=halo_sem.at[1],
        device_id={"grp": lax.rem(me + 1, GRP)}, device_id_type=MESH,
    )

    def send_cot(j, _):
        dest = peer(j)
        pltpu.make_async_remote_copy(
            src_ref=cstage.at[dest], dst_ref=crecv.at[me],
            send_sem=cot_sem.at[0], recv_sem=cot_sem.at[1],
            device_id={"grp": dest}, device_id_type=MESH,
        ).start()
        return 0

    lax.fori_loop(0, GRP - 1, send_cot, 0)
    crecv[me] = cstage[me]
    halo.start()

    for x in (1, 2):
        ld_vol[x].wait()
        by_phase(x)
    for pair in (0, 1):
        pre = products(w1_back, (1,), pair) + products(w1_rest, (2, 3), pair)
        for h in (0, 1):
            activate(1, 2 * pair + h, pre[:, LANES * h : LANES * (h + 1)] + bias_rows)
    act_copy = [exchange_act(0), exchange_act(1)]
    act_copy[1].start()

    ld_vol[0].wait()
    by_phase(0)
    for pair in (0, 1):
        pre = products(w1_rest, (0, 1), pair)
        for h in (0, 1):
            pre_s[0, 2 * pair + h] = pre[:, LANES * h : LANES * (h + 1)] + bias_rows

    pltpu.make_async_copy(
        crecv.at[pl.ds(0, GRP - 1)], crecv.at[pl.ds(0, GRP - 1)], cot_sem.at[1]
    ).wait()
    got = crecv[...].astype(F32)
    for p in (0, 1):
        cotf[p] = got[:, 8 * p : 8 * p + 8].reshape(FILT, LANES).astype(BF16)
    cx = pltpu.make_async_remote_copy(
        src_ref=cotf.at[:, pl.ds(pl.multiple_of(HALF * (1 - core), HALF), HALF), :], dst_ref=cpart,
        send_sem=cx_sem.at[0], recv_sem=cx_sem.at[1],
        device_id={"samp": other}, device_id_type=MESH,
    )
    cx.start()

    my_half = pl.ds(pl.multiple_of(HALF * core, HALF), HALF)

    def second_patch(i, n):
        b, e = COMBOS[n]
        phase = 2 * (b != 0) + (e != 0)
        parts = []
        for ref in (act_own, act_part):
            x = ref[i, phase]
            if b < 0 or e < 0:
                x = x.astype(F32)
                if e < 0:
                    x = z_before(x)
                if b < 0:
                    x = y_before(x)
                x = x.astype(BF16)
            parts.append(x)
        return jnp.concatenate(parts, axis=1)

    contract = (((1,), (1,)), ((), ()))

    def pack(group, taps):
        low = lax.broadcasted_iota(jnp.int32, (16, 8, LANES), 1) < 4
        t = [x.reshape(16, 8, LANES) for x in taps]
        turned = [pltpu.roll(x, 4, 1) for x in t]
        even = [jnp.where(low, t[j], turned[j + 1]) for j in (0, 2)]
        odd = [jnp.where(low, turned[j], t[j + 1]) for j in (0, 2)]
        rows = slice(16 * group, 16 * group + 16)
        send_buf[:, 0, rows, :] = jnp.concatenate(even, axis=1).astype(BF16)
        send_buf[:, 1, rows, :] = jnp.concatenate(odd, axis=1).astype(BF16)

    def send_chunk(which):
        rows = pl.ds(CHUNK_START[which], CHUNK_ROWS[which])

        def body(j, _):
            dest = ring_peer(j)
            pltpu.make_async_remote_copy(
                src_ref=send_buf.at[lax.div(dest, 2), lax.rem(dest, 2), rows],
                dst_ref=recv_buf[which].at[j],
                send_sem=rs_sem.at[0, which], recv_sem=rs_sem.at[1, which],
                device_id={"grp": dest}, device_id_type=MESH,
            ).start()
            return 0

        lax.fori_loop(0, GRP - 1, body, 0)

    def cot_rhs(p):
        return jnp.concatenate([cotf[p, my_half, :], cpart[p]], axis=1)

    act_copy[1].wait_recv()
    cx.wait_recv()
    rhs_both = jnp.concatenate([cot_rhs(0), cot_rhs(1)], axis=0)
    held = []
    for n in range(9):
        d = lax.dot_general(second_patch(1, n), rhs_both, contract, preferred_element_type=F32)
        held += [d[:, :LANES], d[:, LANES:]]
        if len(held) == 4:
            pack(n // 2, held)
            held = []
    carry[0] = held[0]
    carry[1] = held[1]
    send_chunk(0)

    halo.wait_recv()
    for q in range(4):
        activate(0, q, pre_s[0, q] + hrecv[q].astype(F32))
    act_copy[0].start()

    for p in (0, 1):
        turned = jnp.transpose(cotf[p].astype(F32))
        cvar[p, 0] = turned.astype(BF16)
        cvar[p, 2] = row_y_after(turned).astype(BF16)
        after = row_z_after(turned)
        cvar[p, 1] = after.astype(BF16)
        cvar[p, 3] = row_y_after(after).astype(BF16)

    act_copy[0].wait_recv()
    rhs_one = cot_rhs(0)
    held = [carry[0], carry[1]]
    group = 4
    for n in range(9):
        held.append(
            lax.dot_general(second_patch(0, n), rhs_one, contract, preferred_element_type=F32)
        )
        if len(held) == 4:
            pack(group, held)
            group += 1
            held = []
            if group == 6:
                send_chunk(1)
    pack(group, held + [jnp.zeros((CH, LANES), F32)] * (4 - len(held)))
    send_chunk(2)

    ld_w2.wait()
    for i in (0, 1):
        for q, (qy, qz) in enumerate(PHASES):
            left, right = [], []
            for a, p in ((0, 0),) if i == 0 else ((1, 0), (-1, 1)):
                for b, sy in ((0, 0),) if qy == 0 else ((1, 0), (-1, 1)):
                    for e, sz in ((0, 0),) if qz == 0 else ((1, 0), (-1, 1)):
                        left.append(cvar[p, 2 * sy + sz])
                        right.append(w2v[9 * (a + 1) + 3 * (b + 1) + e + 1])
            grad = jnp.dot(
                jnp.concatenate(left, axis=1),
                jnp.concatenate(right, axis=0),
                preferred_element_type=F32,
            )
            grad = jnp.transpose(grad.astype(BF16).astype(F32))
            z = pre_s[i, q]
            g = 1.0 / (1.0 + jnp.exp(-z))
            pgf[pl.ds(4 * i + q, CH, stride=8), :] = grad * (g * (1.0 + z * (1.0 - g)))
    pre_v[...] = pgf[...].reshape(CH, 8, LANES).astype(BF16)
    st_pre = pltpu.make_async_copy(pre_v, pre_out, lsem.at[4])
    st_pre.start()

    mine = send_buf.at[lax.div(me, 2), lax.rem(me, 2)]
    for which in CHUNKS:
        received, parts = recv_buf[which], part_buf[which]
        pltpu.make_async_copy(received, received, rs_sem.at[1, which]).wait()
        parts[samp] = lax.fori_loop(
            0,
            GRP - 1,
            lambda j, acc, received=received: acc + received[j].astype(F32),
            mine[pl.ds(CHUNK_START[which], CHUNK_ROWS[which]), :].astype(F32),
        ).astype(BF16)

        def send_part(j, _, parts=parts, which=which):
            pltpu.make_async_remote_copy(
                src_ref=parts.at[samp], dst_ref=parts.at[samp],
                send_sem=samp_sem.at[0, which], recv_sem=samp_sem.at[1, which],
                device_id={"samp": samp_peer(j)}, device_id_type=MESH,
            ).start()
            return 0

        lax.fori_loop(0, SAMP - 1, send_part, 0)

    for which in CHUNKS:
        parts = part_buf[which]
        seven = parts.at[pl.ds(0, SAMP - 1)]
        pltpu.make_async_copy(seven, seven, samp_sem.at[1, which]).wait()
        for h in (0, 1):
            total = sum(parts[h + 2 * j].astype(F32) for j in range(SAMP // 2)) * SCALE
            first = CHUNK_START[which] // 4
            for slot in range(total.shape[0] // 4):
                if first + slot < TAPS:
                    w2_out[TAP_ORDER[first + slot], :, LANES * h : LANES * (h + 1)] = total[
                        4 * slot : 4 * slot + 4
                    ]

    st_pre.wait()
    halo.wait_send()
    pltpu.make_async_copy(
        cstage.at[pl.ds(0, GRP - 1)], cstage.at[pl.ds(0, GRP - 1)], cot_sem.at[0]
    ).wait()
    cx.wait_send()
    for c in act_copy:
        c.wait_send()
    for which in CHUNKS:
        pltpu.make_async_copy(recv_buf[which], recv_buf[which], rs_sem.at[0, which]).wait()
        seven = part_buf[which].at[pl.ds(0, SAMP - 1)]
        pltpu.make_async_copy(seven, seven, samp_sem.at[0, which]).wait()


def hand_over(pre, w2g, pre_out, w2_out, sem):
    copies = [
        pltpu.make_async_copy(pre, pre_out, sem.at[0]),
        pltpu.make_async_copy(w2g, w2_out, sem.at[1]),
    ]
    for c in copies:
        c.start()
    for c in copies:
        c.wait()


def on_device(volumes, w_first, bias_first, w_second, cotangent):
    hbm = pl.BlockSpec(memory_space=pltpu.HBM)
    vmem = pl.BlockSpec(memory_space=pltpu.VMEM)
    dma = pltpu.SemaphoreType.DMA
    scratch = [
        pltpu.VMEM((4, CIN, 16, LANES), BF16),
        pltpu.VMEM((TAPS * CIN, CH), BF16),
        pltpu.VMEM((CH, K_BACK), BF16),
        pltpu.VMEM((CH, TAPS * CIN - K_BACK), BF16),
        pltpu.VMEM((1, CH), F32),
        pltpu.VMEM((TAPS, FILT, CH), BF16),
        pltpu.VMEM((8, GRP, LANES), BF16),
        pltpu.VMEM((GRP * 16, LANES), F32),
        pltpu.VMEM((GRP, 16, LANES), BF16),
        pltpu.VMEM((GRP, 16, LANES), BF16),
        pltpu.VMEM((2, FILT, LANES), BF16),
        pltpu.VMEM((2, HALF, LANES), BF16),
        pltpu.VMEM((256, 256), BF16),
        pltpu.VMEM((4, 16, CIN, LANES), BF16),
        pltpu.VMEM((4, 4, CIN, LANES), BF16),
        pltpu.VMEM((4, 4, CIN, LANES), BF16),
        pltpu.VMEM((4, CIN, LANES), BF16),
        pltpu.VMEM((4, CH, LANES), BF16),
        pltpu.VMEM((4, CH, LANES), BF16),
        pltpu.VMEM((2, 4, CH, LANES), F32),
        pltpu.VMEM((2, 4, CH, LANES), BF16),
        pltpu.VMEM((2, 4, CH, LANES), BF16),
        pltpu.VMEM((2, CH, LANES), F32),
        pltpu.VMEM((2, 4, LANES, FILT), BF16),
        pltpu.VMEM((CH * 8, LANES), F32),
        pltpu.VMEM((CH, 8, LANES), BF16),
        pltpu.VMEM((GRP // 2, 2, ROWS, LANES), BF16),
        *[pltpu.VMEM((GRP - 1, n, LANES), BF16) for n in CHUNK_ROWS],
        *[pltpu.VMEM((SAMP, n, LANES), BF16) for n in CHUNK_ROWS],
        dma((5,)),
        dma((4,)),
        dma((2,)),
        dma((2,)),
        dma((2,)),
        dma((2, 2)),
        dma((2, len(CHUNK_ROWS))),
        dma((2, len(CHUNK_ROWS))),
    ]

    pre, w2g = pl.pallas_call(
        kernel,
        out_shape=(
            jax.ShapeDtypeStruct((CH, 8, LANES), BF16),
            jax.ShapeDtypeStruct((TAPS, 4, FILT), F32),
        ),
        in_specs=[hbm] * 5,
        out_specs=(hbm, vmem),
        scratch_shapes=scratch,
        compiler_params=pltpu.CompilerParams(
            collective_id=0, has_side_effects=True, vmem_limit_bytes=60 * 1024 * 1024
        ),
        name="layers",
    )(
        volumes[0],
        jnp.transpose(w_first),
        bias_first.reshape(1, CH),
        jnp.transpose(w_second, (1, 0, 2)),
        cotangent[0],
    )
    pre, w2g = pl.pallas_call(
        hand_over,
        out_shape=(
            jax.ShapeDtypeStruct(pre.shape, pre.dtype),
            jax.ShapeDtypeStruct(w2g.shape, w2g.dtype),
        ),
        in_specs=[vmem, vmem],
        out_specs=(hbm, hbm),
        scratch_shapes=[dma((2,))],
        name="hand_over",
    )(pre, w2g)
    return pre.reshape(1, CH, 2, 4, LANES), jnp.transpose(w2g, (2, 0, 1))


def solution(mesh):
    placed = (P("samp", None, "grp", None, None), P(), P(), P(), P("samp", "grp", None, None))
    return jax.shard_map(
        on_device,
        mesh=mesh,
        in_specs=placed,
        out_specs=(P("samp", None, "grp", None, None), P(None, None, "grp")),
        check_vma=False,
    )
```

```python
import math

import jax
import jax.numpy as jnp
from jax import lax
from jax.experimental import pallas as pl
from jax.experimental.pallas import tpu as pltpu
from jax.sharding import PartitionSpec as P

MESH = pl.DeviceIdType.MESH
F32 = jnp.float32
BF16 = jnp.bfloat16

CIN = 64
CH = 128
FILT = 256
HALF = 128
LANES = 128
ZQ = 16
GRP = 32
SAMP = 8
TAPS = 27
COMBOS = [(b, e) for b in (-1, 0, 1) for e in (-1, 0, 1)]
PHASES = [(0, 0), (0, 1), (1, 0), (1, 1)]
TAP_ORDER = [t for n in range(9) for t in (18 + n, n)] + [9 + n for n in range(9)]
CHUNK_ROWS = (64, 32, 16)
CHUNK_START = (0, 64, 96)
CHUNKS = range(len(CHUNK_ROWS))
ROWS = sum(CHUNK_ROWS)
K_BACK = 9 * CIN
SCALE = 1.0 / math.sqrt(32768)


def lane_index(shape):
    return lax.broadcasted_iota(jnp.int32, shape, len(shape) - 1)


def y_before(x):
    return pltpu.roll(x, ZQ, 1)


def z_before(x):
    first = lane_index(x.shape) % ZQ == 0
    return jnp.where(first, pltpu.roll(x, LANES + 1 - ZQ, 1), pltpu.roll(x, 1, 1))


def row_y_after(x):
    return jnp.concatenate([x[ZQ:], x[:ZQ]], axis=0)


def row_z_after(x):
    rows = x.shape[0]
    last = lax.broadcasted_iota(jnp.int32, x.shape, 0) % ZQ == ZQ - 1
    return jnp.where(last, pltpu.roll(x, ZQ - 1, 0), pltpu.roll(x, rows - 1, 0))


def kernel(
    vol, w1t, bias, w2, cot,
    pre_out, w2_out,
    vbuf, w1tv, w1_back, w1_rest, biasv, w2v, cotv, cstg, cstage, crecv, cotf, cpart,
    perm, tn, ty, tz, tyz, hsend, hrecv, pre_s, act_own, act_part, carry, cvar, pgf,
    send_buf, recv_a, recv_b, recv_c, part_a, part_b, part_c,
    lsem, vsem, halo_sem, cot_sem, cx_sem, act_sem, rs_sem, samp_sem,
):
    recv_buf = (recv_a, recv_b, recv_c)
    part_buf = (part_a, part_b, part_c)
    me = lax.axis_index("grp")
    samp = lax.axis_index("samp")
    core = lax.rem(samp, 2)
    other = samp + 1 - 2 * core

    def peer(j):
        def step(v):
            return 2 + lax.div(v * (7 - v), 2)

        z = lax.rem(lax.div(me, 16) + 1 + lax.div(j, 16), 2)
        x = lax.rem(lax.rem(lax.div(me, 4), 4) + step(lax.rem(lax.div(j, 4), 4)), 4)
        y = lax.rem(lax.rem(me, 4) + step(lax.rem(j, 4)), 4)
        return 16 * z + 4 * x + y

    def ring_peer(j):
        return lax.rem(me + 1 + j, GRP)

    def samp_peer(j):
        return lax.rem(samp + 4 + j + lax.div(j, 4), SAMP)

    ld_cot = pltpu.make_async_copy(cot, cotv, lsem.at[0])
    ld_w1 = pltpu.make_async_copy(w1t, w1tv, lsem.at[1])
    ld_bias = pltpu.make_async_copy(bias, biasv, lsem.at[2])
    ld_w2 = pltpu.make_async_copy(w2, w2v, lsem.at[3])
    ld_vol = [pltpu.make_async_copy(vol.at[:, x], vbuf.at[x], vsem.at[x]) for x in range(4)]
    ld_cot.start()
    ld_w1.start()
    ld_bias.start()
    for x in (3, 1, 2, 0):
        ld_vol[x].start()
    ld_w2.start()

    barrier = pltpu.get_barrier_semaphore()

    def greet_grp(j, _):
        pl.semaphore_signal(barrier, inc=1, device_id={"grp": peer(j)}, device_id_type=MESH)
        return 0

    def greet_samp(j, _):
        pl.semaphore_signal(barrier, inc=1, device_id={"samp": samp_peer(j)}, device_id_type=MESH)
        return 0

    lax.fori_loop(0, SAMP - 1, greet_samp, 0)
    lax.fori_loop(0, GRP - 1, greet_grp, 0)

    ld_cot.wait()
    for f in range(8):
        x = cotv[f].astype(F32)
        cstg[pl.ds(f, GRP, stride=16), :] = x
        cstg[pl.ds(8 + f, GRP, stride=16), :] = jnp.concatenate([x[1:], x[:1]], axis=0)
    cstage[...] = cstg[...].reshape(GRP, 16, LANES).astype(BF16)

    pl.semaphore_wait(barrier, GRP - 1 + SAMP - 1)

    halo = pltpu.make_async_remote_copy(
        src_ref=hsend, dst_ref=hrecv,
        send_sem=halo_sem.at[0], recv_sem=halo_sem.at[1],
        device_id={"grp": lax.rem(me + 1, GRP)}, device_id_type=MESH,
    )

    def send_cot(j, _):
        dest = peer(j)
        pltpu.make_async_remote_copy(
            src_ref=cstage.at[dest], dst_ref=crecv.at[me],
            send_sem=cot_sem.at[0], recv_sem=cot_sem.at[1],
            device_id={"grp": dest}, device_id_type=MESH,
        ).start()
        return 0

    lax.fori_loop(0, GRP - 1, send_cot, 0)
    crecv[me] = cstage[me]

    ld_w1.wait()
    ld_bias.wait()
    w1_back[...] = jnp.transpose(w1tv[:K_BACK, :])
    w1_rest[...] = jnp.transpose(w1tv[K_BACK:, :])
    bias_rows = jnp.transpose(jnp.broadcast_to(biasv[...], (CH, CH)))
    row = lax.broadcasted_iota(jnp.int32, (256, 256), 0)
    col = lax.broadcasted_iota(jnp.int32, (256, 256), 1)
    perm[...] = jnp.where(col == (row % 16) * 16 + row // 16, 1.0, 0.0).astype(BF16)

    def by_phase(x):
        for blk in range(4):
            rows = vbuf[x, 16 * blk : 16 * blk + 16].reshape(256, LANES)
            moved = jnp.dot(perm[...], rows, preferred_element_type=F32)
            here = slice(16 * blk, 16 * blk + 16)
            tn[x, :, here, :] = moved.reshape(16, 16, LANES).astype(BF16)
            ty[x, :, here, :] = y_before(moved[192:256]).reshape(4, 16, LANES).astype(BF16)
            ends = jnp.concatenate([moved[64 * r + 48 : 64 * r + 64] for r in range(4)], axis=0)
            ends = z_before(ends)
            tz[x, :, here, :] = ends.reshape(4, 16, LANES).astype(BF16)
            tyz[x, here, :] = y_before(ends[48:64]).astype(BF16)

    def patch(x, qy, qz, b, e):
        along_y, along_z = 2 * qy + b, 2 * qz + e
        ry, rz = along_y % 4, along_z % 4
        if along_y < 0 and along_z < 0:
            return tyz[x]
        if along_y < 0:
            return ty[x, rz]
        if along_z < 0:
            return tz[x, ry]
        return tn[x, 4 * ry + rz]

    def products(weights, planes, pair):
        columns = []
        for q in (2 * pair, 2 * pair + 1):
            qy, qz = PHASES[q]
            columns.append(
                jnp.concatenate([patch(x, qy, qz, b, e) for x in planes for b, e in COMBOS], axis=0)
            )
        return jnp.dot(
            weights[...], jnp.concatenate(columns, axis=1), preferred_element_type=F32
        )

    def activate(i, q, z):
        pre_s[i, q] = z
        act_own[i, q] = (z / (1.0 + jnp.exp(-z))).astype(BF16)

    def exchange_act(i):
        return pltpu.make_async_remote_copy(
            src_ref=act_own.at[i], dst_ref=act_part.at[i],
            send_sem=act_sem.at[0, i], recv_sem=act_sem.at[1, i],
            device_id={"samp": other}, device_id_type=MESH,
        )

    ld_vol[3].wait()
    by_phase(3)
    for pair in (0, 1):
        back = products(w1_back, (3,), pair).astype(BF16)
        hsend[2 * pair] = back[:, :LANES]
        hsend[2 * pair + 1] = back[:, LANES:]
    halo.start()

    for x in (1, 2):
        ld_vol[x].wait()
        by_phase(x)
    for pair in (0, 1):
        pre = products(w1_back, (1,), pair) + products(w1_rest, (2, 3), pair)
        for h in (0, 1):
            activate(1, 2 * pair + h, pre[:, LANES * h : LANES * (h + 1)] + bias_rows)
    act_copy = [exchange_act(0), exchange_act(1)]
    act_copy[1].start()

    ld_vol[0].wait()
    by_phase(0)
    for pair in (0, 1):
        pre = products(w1_rest, (0, 1), pair)
        for h in (0, 1):
            pre_s[0, 2 * pair + h] = pre[:, LANES * h : LANES * (h + 1)] + bias_rows

    pltpu.make_async_copy(
        crecv.at[pl.ds(0, GRP - 1)], crecv.at[pl.ds(0, GRP - 1)], cot_sem.at[1]
    ).wait()
    got = crecv[...].astype(F32)
    for p in (0, 1):
        cotf[p] = got[:, 8 * p : 8 * p + 8].reshape(FILT, LANES).astype(BF16)
    cx = pltpu.make_async_remote_copy(
        src_ref=cotf.at[:, pl.ds(pl.multiple_of(HALF * (1 - core), HALF), HALF), :], dst_ref=cpart,
        send_sem=cx_sem.at[0], recv_sem=cx_sem.at[1],
        device_id={"samp": other}, device_id_type=MESH,
    )
    cx.start()

    my_half = pl.ds(pl.multiple_of(HALF * core, HALF), HALF)

    def second_patch(i, n):
        b, e = COMBOS[n]
        phase = 2 * (b != 0) + (e != 0)
        parts = []
        for ref in (act_own, act_part):
            x = ref[i, phase]
            if b < 0 or e < 0:
                x = x.astype(F32)
                if e < 0:
                    x = z_before(x)
                if b < 0:
                    x = y_before(x)
                x = x.astype(BF16)
            parts.append(x)
        return jnp.concatenate(parts, axis=1)

    contract = (((1,), (1,)), ((), ()))

    def pack(group, taps):
        low = lax.broadcasted_iota(jnp.int32, (16, 8, LANES), 1) < 4
        t = [x.reshape(16, 8, LANES) for x in taps]
        turned = [pltpu.roll(x, 4, 1) for x in t]
        even = [jnp.where(low, t[j], turned[j + 1]) for j in (0, 2)]
        odd = [jnp.where(low, turned[j], t[j + 1]) for j in (0, 2)]
        rows = slice(16 * group, 16 * group + 16)
        send_buf[:, 0, rows, :] = jnp.concatenate(even, axis=1).astype(BF16)
        send_buf[:, 1, rows, :] = jnp.concatenate(odd, axis=1).astype(BF16)

    def send_chunk(which):
        rows = pl.ds(CHUNK_START[which], CHUNK_ROWS[which])

        def body(j, _):
            dest = ring_peer(j)
            pltpu.make_async_remote_copy(
                src_ref=send_buf.at[lax.div(dest, 2), lax.rem(dest, 2), rows],
                dst_ref=recv_buf[which].at[j],
                send_sem=rs_sem.at[0, which], recv_sem=rs_sem.at[1, which],
                device_id={"grp": dest}, device_id_type=MESH,
            ).start()
            return 0

        lax.fori_loop(0, GRP - 1, body, 0)

    def cot_rhs(p):
        return jnp.concatenate([cotf[p, my_half, :], cpart[p]], axis=1)

    act_copy[1].wait_recv()
    cx.wait_recv()
    rhs_both = jnp.concatenate([cot_rhs(0), cot_rhs(1)], axis=0)
    held = []
    for n in range(9):
        d = lax.dot_general(second_patch(1, n), rhs_both, contract, preferred_element_type=F32)
        held += [d[:, :LANES], d[:, LANES:]]
        if len(held) == 4:
            pack(n // 2, held)
            held = []
    carry[0] = held[0]
    carry[1] = held[1]
    send_chunk(0)

    halo.wait_recv()
    for q in range(4):
        activate(0, q, pre_s[0, q] + hrecv[q].astype(F32))
    act_copy[0].start()

    for p in (0, 1):
        turned = jnp.transpose(cotf[p].astype(F32))
        cvar[p, 0] = turned.astype(BF16)
        cvar[p, 2] = row_y_after(turned).astype(BF16)
        after = row_z_after(turned)
        cvar[p, 1] = after.astype(BF16)
        cvar[p, 3] = row_y_after(after).astype(BF16)

    act_copy[0].wait_recv()
    rhs_one = cot_rhs(0)
    held = [carry[0], carry[1]]
    group = 4
    for n in range(9):
        held.append(
            lax.dot_general(second_patch(0, n), rhs_one, contract, preferred_element_type=F32)
        )
        if len(held) == 4:
            pack(group, held)
            group += 1
            held = []
            if group == 6:
                send_chunk(1)
    pack(group, held + [jnp.zeros((CH, LANES), F32)] * (4 - len(held)))
    send_chunk(2)

    ld_w2.wait()
    for i in (0, 1):
        for q, (qy, qz) in enumerate(PHASES):
            left, right = [], []
            for a, p in ((0, 0),) if i == 0 else ((1, 0), (-1, 1)):
                for b, sy in ((0, 0),) if qy == 0 else ((1, 0), (-1, 1)):
                    for e, sz in ((0, 0),) if qz == 0 else ((1, 0), (-1, 1)):
                        left.append(cvar[p, 2 * sy + sz])
                        right.append(w2v[9 * (a + 1) + 3 * (b + 1) + e + 1])
            grad = jnp.dot(
                jnp.concatenate(left, axis=1),
                jnp.concatenate(right, axis=0),
                preferred_element_type=F32,
            )
            grad = jnp.transpose(grad.astype(BF16).astype(F32))
            z = pre_s[i, q]
            g = 1.0 / (1.0 + jnp.exp(-z))
            pgf[pl.ds(4 * i + q, CH, stride=8), :] = grad * (g * (1.0 + z * (1.0 - g)))
    pre_out[...] = pgf[...].reshape(CH, 8, LANES).astype(BF16)

    mine = send_buf.at[lax.div(me, 2), lax.rem(me, 2)]
    for which in CHUNKS:
        received, parts = recv_buf[which], part_buf[which]
        pltpu.make_async_copy(received, received, rs_sem.at[1, which]).wait()
        parts[samp] = lax.fori_loop(
            0,
            GRP - 1,
            lambda j, acc, received=received: acc + received[j].astype(F32),
            mine[pl.ds(CHUNK_START[which], CHUNK_ROWS[which]), :].astype(F32),
        ).astype(BF16)

        def send_part(j, _, parts=parts, which=which):
            pltpu.make_async_remote_copy(
                src_ref=parts.at[samp], dst_ref=parts.at[samp],
                send_sem=samp_sem.at[0, which], recv_sem=samp_sem.at[1, which],
                device_id={"samp": samp_peer(j)}, device_id_type=MESH,
            ).start()
            return 0

        lax.fori_loop(0, SAMP - 1, send_part, 0)

    for which in CHUNKS:
        parts = part_buf[which]
        seven = parts.at[pl.ds(0, SAMP - 1)]
        pltpu.make_async_copy(seven, seven, samp_sem.at[1, which]).wait()
        for h in (0, 1):
            total = sum(parts[h + 2 * j].astype(F32) for j in range(SAMP // 2)) * SCALE
            first = CHUNK_START[which] // 4
            for slot in range(total.shape[0] // 4):
                if first + slot < TAPS:
                    w2_out[TAP_ORDER[first + slot], :, LANES * h : LANES * (h + 1)] = total[
                        4 * slot : 4 * slot + 4
                    ]

    halo.wait_send()
    pltpu.make_async_copy(
        cstage.at[pl.ds(0, GRP - 1)], cstage.at[pl.ds(0, GRP - 1)], cot_sem.at[0]
    ).wait()
    cx.wait_send()
    for c in act_copy:
        c.wait_send()
    for which in CHUNKS:
        pltpu.make_async_copy(recv_buf[which], recv_buf[which], rs_sem.at[0, which]).wait()
        seven = part_buf[which].at[pl.ds(0, SAMP - 1)]
        pltpu.make_async_copy(seven, seven, samp_sem.at[0, which]).wait()


def hand_over(pre, w2g, pre_out, w2_out, sem):
    copies = [
        pltpu.make_async_copy(pre, pre_out, sem.at[0]),
        pltpu.make_async_copy(w2g, w2_out, sem.at[1]),
    ]
    for c in copies:
        c.start()
    for c in copies:
        c.wait()


def on_device(volumes, w_first, bias_first, w_second, cotangent):
    hbm = pl.BlockSpec(memory_space=pltpu.HBM)
    vmem = pl.BlockSpec(memory_space=pltpu.VMEM)
    dma = pltpu.SemaphoreType.DMA
    scratch = [
        pltpu.VMEM((4, CIN, 16, LANES), BF16),
        pltpu.VMEM((TAPS * CIN, CH), BF16),
        pltpu.VMEM((CH, K_BACK), BF16),
        pltpu.VMEM((CH, TAPS * CIN - K_BACK), BF16),
        pltpu.VMEM((1, CH), F32),
        pltpu.VMEM((TAPS, FILT, CH), BF16),
        pltpu.VMEM((8, GRP, LANES), BF16),
        pltpu.VMEM((GRP * 16, LANES), F32),
        pltpu.VMEM((GRP, 16, LANES), BF16),
        pltpu.VMEM((GRP, 16, LANES), BF16),
        pltpu.VMEM((2, FILT, LANES), BF16),
        pltpu.VMEM((2, HALF, LANES), BF16),
        pltpu.VMEM((256, 256), BF16),
        pltpu.VMEM((4, 16, CIN, LANES), BF16),
        pltpu.VMEM((4, 4, CIN, LANES), BF16),
        pltpu.VMEM((4, 4, CIN, LANES), BF16),
        pltpu.VMEM((4, CIN, LANES), BF16),
        pltpu.VMEM((4, CH, LANES), BF16),
        pltpu.VMEM((4, CH, LANES), BF16),
        pltpu.VMEM((2, 4, CH, LANES), F32),
        pltpu.VMEM((2, 4, CH, LANES), BF16),
        pltpu.VMEM((2, 4, CH, LANES), BF16),
        pltpu.VMEM((2, CH, LANES), F32),
        pltpu.VMEM((2, 4, LANES, FILT), BF16),
        pltpu.VMEM((CH * 8, LANES), F32),
        pltpu.VMEM((GRP // 2, 2, ROWS, LANES), BF16),
        *[pltpu.VMEM((GRP - 1, n, LANES), BF16) for n in CHUNK_ROWS],
        *[pltpu.VMEM((SAMP, n, LANES), BF16) for n in CHUNK_ROWS],
        dma((4,)),
        dma((4,)),
        dma((2,)),
        dma((2,)),
        dma((2,)),
        dma((2, 2)),
        dma((2, len(CHUNK_ROWS))),
        dma((2, len(CHUNK_ROWS))),
    ]

    pre, w2g = pl.pallas_call(
        kernel,
        out_shape=(
            pltpu.VMEM((CH, 8, LANES), BF16),
            pltpu.VMEM((TAPS, 4, FILT), F32),
        ),
        in_specs=[hbm] * 5,
        out_specs=(vmem, vmem),
        scratch_shapes=scratch,
        compiler_params=pltpu.CompilerParams(
            collective_id=0, has_side_effects=True, vmem_limit_bytes=60 * 1024 * 1024
        ),
        name="layers",
    )(
        volumes[0],
        jnp.transpose(w_first),
        bias_first.reshape(1, CH),
        jnp.transpose(w_second, (1, 0, 2)),
        cotangent[0],
    )
    pre, w2g = pl.pallas_call(
        hand_over,
        out_shape=(
            jax.ShapeDtypeStruct(pre.shape, pre.dtype),
            jax.ShapeDtypeStruct(w2g.shape, w2g.dtype),
        ),
        in_specs=[vmem, vmem],
        out_specs=(hbm, hbm),
        scratch_shapes=[dma((2,))],
        name="hand_over",
    )(
        pltpu.with_memory_space_constraint(pre, pltpu.VMEM),
        pltpu.with_memory_space_constraint(w2g, pltpu.VMEM),
    )
    return pre.reshape(1, CH, 2, 4, LANES), jnp.transpose(w2g, (2, 0, 1))


def solution(mesh):
    placed = (P("samp", None, "grp", None, None), P(), P(), P(), P("samp", "grp", None, None))
    return jax.shard_map(
        on_device,
        mesh=mesh,
        in_specs=placed,
        out_specs=(P("samp", None, "grp", None, None), P(None, None, "grp")),
        check_vma=False,
    )
```

```python
import math

import jax
import jax.numpy as jnp
from jax import lax
from jax.experimental import pallas as pl
from jax.experimental.pallas import tpu as pltpu
from jax.sharding import PartitionSpec as P

MESH = pl.DeviceIdType.MESH
F32 = jnp.float32
BF16 = jnp.bfloat16

CIN = 64
CH = 128
FILT = 256
HALF = 128
LANES = 128
ZQ = 16
GRP = 32
SAMP = 8
TAPS = 27
COMBOS = [(b, e) for b in (-1, 0, 1) for e in (-1, 0, 1)]
PHASES = [(0, 0), (0, 1), (1, 0), (1, 1)]
TAP_ORDER = [t for n in range(9) for t in (18 + n, n)] + [9 + n for n in range(9)]
CHUNK_ROWS = (64, 32, 16)
CHUNK_START = (0, 64, 96)
CHUNKS = range(len(CHUNK_ROWS))
ROWS = sum(CHUNK_ROWS)
K_BACK = 9 * CIN
SCALE = 1.0 / math.sqrt(32768)


def lane_index(shape):
    return lax.broadcasted_iota(jnp.int32, shape, len(shape) - 1)


def y_before(x):
    return pltpu.roll(x, ZQ, 1)


def z_before(x):
    first = lane_index(x.shape) % ZQ == 0
    return jnp.where(first, pltpu.roll(x, LANES + 1 - ZQ, 1), pltpu.roll(x, 1, 1))


def row_y_after(x):
    return jnp.concatenate([x[ZQ:], x[:ZQ]], axis=0)


def row_z_after(x):
    rows = x.shape[0]
    last = lax.broadcasted_iota(jnp.int32, x.shape, 0) % ZQ == ZQ - 1
    return jnp.where(last, pltpu.roll(x, ZQ - 1, 0), pltpu.roll(x, rows - 1, 0))


def kernel(
    vol, w1t, bias, w2, cot,
    pre_out, w2_out,
    vbuf, w1tv, w1_back, w1_rest, biasv, w2v, cotv, cstg, cstage, crecv, cotf, cpart,
    perm, tn, ty, tz, tyz, hsend, hrecv, pre_s, act_own, act_part, carry, cvar, pgf,
    send_buf, recv_a, recv_b, recv_c, part_a, part_b, part_c,
    lsem, vsem, halo_sem, cot_sem, cx_sem, act_sem, rs_sem, samp_sem,
):
    recv_buf = (recv_a, recv_b, recv_c)
    part_buf = (part_a, part_b, part_c)
    me = lax.axis_index("grp")
    samp = lax.axis_index("samp")
    core = lax.rem(samp, 2)
    other = samp + 1 - 2 * core

    def peer(j):
        def step(v):
            return 2 + lax.div(v * (7 - v), 2)

        z = lax.rem(lax.div(me, 16) + 1 + lax.div(j, 16), 2)
        x = lax.rem(lax.rem(lax.div(me, 4), 4) + step(lax.rem(lax.div(j, 4), 4)), 4)
        y = lax.rem(lax.rem(me, 4) + step(lax.rem(j, 4)), 4)
        return 16 * z + 4 * x + y

    def ring_peer(j):
        return lax.rem(me + 1 + j, GRP)

    def samp_peer(j):
        return lax.rem(samp + 4 + j + lax.div(j, 4), SAMP)

    ld_cot = pltpu.make_async_copy(cot, cotv, lsem.at[0])
    ld_w1 = pltpu.make_async_copy(w1t, w1tv, lsem.at[1])
    ld_bias = pltpu.make_async_copy(bias, biasv, lsem.at[2])
    ld_w2 = pltpu.make_async_copy(w2, w2v, lsem.at[3])
    ld_vol = [pltpu.make_async_copy(vol.at[:, x], vbuf.at[x], vsem.at[x]) for x in range(4)]
    ld_cot.start()
    ld_w1.start()
    ld_bias.start()
    for x in (3, 1, 2, 0):
        ld_vol[x].start()
    ld_w2.start()

    barrier = pltpu.get_barrier_semaphore()

    def greet_grp(j, _):
        pl.semaphore_signal(barrier, inc=1, device_id={"grp": ring_peer(j)}, device_id_type=MESH)
        return 0

    def greet_samp(j, _):
        pl.semaphore_signal(barrier, inc=1, device_id={"samp": samp_peer(j)}, device_id_type=MESH)
        return 0

    lax.fori_loop(0, SAMP - 1, greet_samp, 0)
    lax.fori_loop(0, GRP - 1, greet_grp, 0)

    ld_cot.wait()
    for f in range(8):
        x = cotv[f].astype(F32)
        cstg[pl.ds(f, GRP, stride=16), :] = x
        cstg[pl.ds(8 + f, GRP, stride=16), :] = jnp.concatenate([x[1:], x[:1]], axis=0)
    cstage[...] = cstg[...].reshape(GRP, 16, LANES).astype(BF16)

    pl.semaphore_wait(barrier, GRP - 1 + SAMP - 1)

    halo = pltpu.make_async_remote_copy(
        src_ref=hsend, dst_ref=hrecv,
        send_sem=halo_sem.at[0], recv_sem=halo_sem.at[1],
        device_id={"grp": lax.rem(me + 1, GRP)}, device_id_type=MESH,
    )

    def send_cot(j, _):
        dest = peer(j)
        pltpu.make_async_remote_copy(
            src_ref=cstage.at[dest], dst_ref=crecv.at[me],
            send_sem=cot_sem.at[0], recv_sem=cot_sem.at[1],
            device_id={"grp": dest}, device_id_type=MESH,
        ).start()
        return 0

    lax.fori_loop(0, GRP - 1, send_cot, 0)
    crecv[me] = cstage[me]

    ld_w1.wait()
    ld_bias.wait()
    w1_back[...] = jnp.transpose(w1tv[:K_BACK, :])
    w1_rest[...] = jnp.transpose(w1tv[K_BACK:, :])
    bias_rows = jnp.transpose(jnp.broadcast_to(biasv[...], (CH, CH)))
    row = lax.broadcasted_iota(jnp.int32, (256, 256), 0)
    col = lax.broadcasted_iota(jnp.int32, (256, 256), 1)
    perm[...] = jnp.where(col == (row % 16) * 16 + row // 16, 1.0, 0.0).astype(BF16)

    def by_phase(x):
        for blk in range(4):
            rows = vbuf[x, 16 * blk : 16 * blk + 16].reshape(256, LANES)
            moved = jnp.dot(perm[...], rows, preferred_element_type=F32)
            here = slice(16 * blk, 16 * blk + 16)
            tn[x, :, here, :] = moved.reshape(16, 16, LANES).astype(BF16)
            ty[x, :, here, :] = y_before(moved[192:256]).reshape(4, 16, LANES).astype(BF16)
            ends = jnp.concatenate([moved[64 * r + 48 : 64 * r + 64] for r in range(4)], axis=0)
            ends = z_before(ends)
            tz[x, :, here, :] = ends.reshape(4, 16, LANES).astype(BF16)
            tyz[x, here, :] = y_before(ends[48:64]).astype(BF16)

    def patch(x, qy, qz, b, e):
        along_y, along_z = 2 * qy + b, 2 * qz + e
        ry, rz = along_y % 4, along_z % 4
        if along_y < 0 and along_z < 0:
            return tyz[x]
        if along_y < 0:
            return ty[x, rz]
        if along_z < 0:
            return tz[x, ry]
        return tn[x, 4 * ry + rz]

    def products(weights, planes, pair):
        columns = []
        for q in (2 * pair, 2 * pair + 1):
            qy, qz = PHASES[q]
            columns.append(
                jnp.concatenate([patch(x, qy, qz, b, e) for x in planes for b, e in COMBOS], axis=0)
            )
        return jnp.dot(
            weights[...], jnp.concatenate(columns, axis=1), preferred_element_type=F32
        )

    def activate(i, q, z):
        pre_s[i, q] = z
        act_own[i, q] = (z / (1.0 + jnp.exp(-z))).astype(BF16)

    def exchange_act(i):
        return pltpu.make_async_remote_copy(
            src_ref=act_own.at[i], dst_ref=act_part.at[i],
            send_sem=act_sem.at[0, i], recv_sem=act_sem.at[1, i],
            device_id={"samp": other}, device_id_type=MESH,
        )

    ld_vol[3].wait()
    by_phase(3)
    for pair in (0, 1):
        back = products(w1_back, (3,), pair).astype(BF16)
        hsend[2 * pair] = back[:, :LANES]
        hsend[2 * pair + 1] = back[:, LANES:]
    halo.start()

    for x in (1, 2):
        ld_vol[x].wait()
        by_phase(x)
    for pair in (0, 1):
        pre = products(w1_back, (1,), pair) + products(w1_rest, (2, 3), pair)
        for h in (0, 1):
            activate(1, 2 * pair + h, pre[:, LANES * h : LANES * (h + 1)] + bias_rows)
    act_copy = [exchange_act(0), exchange_act(1)]
    act_copy[1].start()

    ld_vol[0].wait()
    by_phase(0)
    for pair in (0, 1):
        pre = products(w1_rest, (0, 1), pair)
        for h in (0, 1):
            pre_s[0, 2 * pair + h] = pre[:, LANES * h : LANES * (h + 1)] + bias_rows

    pltpu.make_async_copy(
        crecv.at[pl.ds(0, GRP - 1)], crecv.at[pl.ds(0, GRP - 1)], cot_sem.at[1]
    ).wait()
    got = crecv[...].astype(F32)
    for p in (0, 1):
        cotf[p] = got[:, 8 * p : 8 * p + 8].reshape(FILT, LANES).astype(BF16)
    cx = pltpu.make_async_remote_copy(
        src_ref=cotf.at[:, pl.ds(pl.multiple_of(HALF * (1 - core), HALF), HALF), :], dst_ref=cpart,
        send_sem=cx_sem.at[0], recv_sem=cx_sem.at[1],
        device_id={"samp": other}, device_id_type=MESH,
    )
    cx.start()

    my_half = pl.ds(pl.multiple_of(HALF * core, HALF), HALF)

    def second_patch(i, n):
        b, e = COMBOS[n]
        phase = 2 * (b != 0) + (e != 0)
        parts = []
        for ref in (act_own, act_part):
            x = ref[i, phase]
            if b < 0 or e < 0:
                x = x.astype(F32)
                if e < 0:
                    x = z_before(x)
                if b < 0:
                    x = y_before(x)
                x = x.astype(BF16)
            parts.append(x)
        return jnp.concatenate(parts, axis=1)

    contract = (((1,), (1,)), ((), ()))

    def pack(group, taps):
        low = lax.broadcasted_iota(jnp.int32, (16, 8, LANES), 1) < 4
        t = [x.reshape(16, 8, LANES) for x in taps]
        turned = [pltpu.roll(x, 4, 1) for x in t]
        even = [jnp.where(low, t[j], turned[j + 1]) for j in (0, 2)]
        odd = [jnp.where(low, turned[j], t[j + 1]) for j in (0, 2)]
        rows = slice(16 * group, 16 * group + 16)
        send_buf[:, 0, rows, :] = jnp.concatenate(even, axis=1).astype(BF16)
        send_buf[:, 1, rows, :] = jnp.concatenate(odd, axis=1).astype(BF16)

    def send_chunk(which):
        rows = pl.ds(CHUNK_START[which], CHUNK_ROWS[which])

        def body(j, _):
            dest = ring_peer(j)
            pltpu.make_async_remote_copy(
                src_ref=send_buf.at[lax.div(dest, 2), lax.rem(dest, 2), rows],
                dst_ref=recv_buf[which].at[j],
                send_sem=rs_sem.at[0, which], recv_sem=rs_sem.at[1, which],
                device_id={"grp": dest}, device_id_type=MESH,
            ).start()
            return 0

        lax.fori_loop(0, GRP - 1, body, 0)

    def cot_rhs(p):
        return jnp.concatenate([cotf[p, my_half, :], cpart[p]], axis=1)

    act_copy[1].wait_recv()
    cx.wait_recv()
    rhs_both = jnp.concatenate([cot_rhs(0), cot_rhs(1)], axis=0)
    held = []
    for n in range(9):
        d = lax.dot_general(second_patch(1, n), rhs_both, contract, preferred_element_type=F32)
        held += [d[:, :LANES], d[:, LANES:]]
        if len(held) == 4:
            pack(n // 2, held)
            held = []
    carry[0] = held[0]
    carry[1] = held[1]
    send_chunk(0)

    halo.wait_recv()
    for q in range(4):
        activate(0, q, pre_s[0, q] + hrecv[q].astype(F32))
    act_copy[0].start()

    for p in (0, 1):
        turned = jnp.transpose(cotf[p].astype(F32))
        cvar[p, 0] = turned.astype(BF16)
        cvar[p, 2] = row_y_after(turned).astype(BF16)
        after = row_z_after(turned)
        cvar[p, 1] = after.astype(BF16)
        cvar[p, 3] = row_y_after(after).astype(BF16)

    act_copy[0].wait_recv()
    rhs_one = cot_rhs(0)
    held = [carry[0], carry[1]]
    group = 4
    for n in range(9):
        held.append(
            lax.dot_general(second_patch(0, n), rhs_one, contract, preferred_element_type=F32)
        )
        if len(held) == 4:
            pack(group, held)
            group += 1
            held = []
            if group == 6:
                send_chunk(1)
    pack(group, held + [jnp.zeros((CH, LANES), F32)] * (4 - len(held)))
    send_chunk(2)

    ld_w2.wait()
    for i in (0, 1):
        for q, (qy, qz) in enumerate(PHASES):
            left, right = [], []
            for a, p in ((0, 0),) if i == 0 else ((1, 0), (-1, 1)):
                for b, sy in ((0, 0),) if qy == 0 else ((1, 0), (-1, 1)):
                    for e, sz in ((0, 0),) if qz == 0 else ((1, 0), (-1, 1)):
                        left.append(cvar[p, 2 * sy + sz])
                        right.append(w2v[9 * (a + 1) + 3 * (b + 1) + e + 1])
            grad = jnp.dot(
                jnp.concatenate(left, axis=1),
                jnp.concatenate(right, axis=0),
                preferred_element_type=F32,
            )
            grad = jnp.transpose(grad.astype(BF16).astype(F32))
            z = pre_s[i, q]
            g = 1.0 / (1.0 + jnp.exp(-z))
            pgf[pl.ds(4 * i + q, CH, stride=8), :] = grad * (g * (1.0 + z * (1.0 - g)))
    pre_out[...] = pgf[...].reshape(CH, 8, LANES).astype(BF16)

    mine = send_buf.at[lax.div(me, 2), lax.rem(me, 2)]
    for which in CHUNKS:
        received, parts = recv_buf[which], part_buf[which]
        pltpu.make_async_copy(received, received, rs_sem.at[1, which]).wait()
        parts[samp] = lax.fori_loop(
            0,
            GRP - 1,
            lambda j, acc, received=received: acc + received[j].astype(F32),
            mine[pl.ds(CHUNK_START[which], CHUNK_ROWS[which]), :].astype(F32),
        ).astype(BF16)

        def send_part(j, _, parts=parts, which=which):
            pltpu.make_async_remote_copy(
                src_ref=parts.at[samp], dst_ref=parts.at[samp],
                send_sem=samp_sem.at[0, which], recv_sem=samp_sem.at[1, which],
                device_id={"samp": samp_peer(j)}, device_id_type=MESH,
            ).start()
            return 0

        lax.fori_loop(0, SAMP - 1, send_part, 0)

    for which in CHUNKS:
        parts = part_buf[which]
        seven = parts.at[pl.ds(0, SAMP - 1)]
        pltpu.make_async_copy(seven, seven, samp_sem.at[1, which]).wait()
        for h in (0, 1):
            total = sum(parts[h + 2 * j].astype(F32) for j in range(SAMP // 2)) * SCALE
            first = CHUNK_START[which] // 4
            for slot in range(total.shape[0] // 4):
                if first + slot < TAPS:
                    w2_out[TAP_ORDER[first + slot], :, LANES * h : LANES * (h + 1)] = total[
                        4 * slot : 4 * slot + 4
                    ]

    halo.wait_send()
    pltpu.make_async_copy(
        cstage.at[pl.ds(0, GRP - 1)], cstage.at[pl.ds(0, GRP - 1)], cot_sem.at[0]
    ).wait()
    cx.wait_send()
    for c in act_copy:
        c.wait_send()
    for which in CHUNKS:
        pltpu.make_async_copy(recv_buf[which], recv_buf[which], rs_sem.at[0, which]).wait()
        seven = part_buf[which].at[pl.ds(0, SAMP - 1)]
        pltpu.make_async_copy(seven, seven, samp_sem.at[0, which]).wait()


def hand_over(pre, w2g, pre_out, w2_out, sem):
    copies = [
        pltpu.make_async_copy(pre, pre_out, sem.at[0]),
        pltpu.make_async_copy(w2g, w2_out, sem.at[1]),
    ]
    for c in copies:
        c.start()
    for c in copies:
        c.wait()


def on_device(volumes, w_first, bias_first, w_second, cotangent):
    hbm = pl.BlockSpec(memory_space=pltpu.HBM)
    vmem = pl.BlockSpec(memory_space=pltpu.VMEM)
    dma = pltpu.SemaphoreType.DMA
    scratch = [
        pltpu.VMEM((4, CIN, 16, LANES), BF16),
        pltpu.VMEM((TAPS * CIN, CH), BF16),
        pltpu.VMEM((CH, K_BACK), BF16),
        pltpu.VMEM((CH, TAPS * CIN - K_BACK), BF16),
        pltpu.VMEM((1, CH), F32),
        pltpu.VMEM((TAPS, FILT, CH), BF16),
        pltpu.VMEM((8, GRP, LANES), BF16),
        pltpu.VMEM((GRP * 16, LANES), F32),
        pltpu.VMEM((GRP, 16, LANES), BF16),
        pltpu.VMEM((GRP, 16, LANES), BF16),
        pltpu.VMEM((2, FILT, LANES), BF16),
        pltpu.VMEM((2, HALF, LANES), BF16),
        pltpu.VMEM((256, 256), BF16),
        pltpu.VMEM((4, 16, CIN, LANES), BF16),
        pltpu.VMEM((4, 4, CIN, LANES), BF16),
        pltpu.VMEM((4, 4, CIN, LANES), BF16),
        pltpu.VMEM((4, CIN, LANES), BF16),
        pltpu.VMEM((4, CH, LANES), BF16),
        pltpu.VMEM((4, CH, LANES), BF16),
        pltpu.VMEM((2, 4, CH, LANES), F32),
        pltpu.VMEM((2, 4, CH, LANES), BF16),
        pltpu.VMEM((2, 4, CH, LANES), BF16),
        pltpu.VMEM((2, CH, LANES), F32),
        pltpu.VMEM((2, 4, LANES, FILT), BF16),
        pltpu.VMEM((CH * 8, LANES), F32),
        pltpu.VMEM((GRP // 2, 2, ROWS, LANES), BF16),
        *[pltpu.VMEM((GRP - 1, n, LANES), BF16) for n in CHUNK_ROWS],
        *[pltpu.VMEM((SAMP, n, LANES), BF16) for n in CHUNK_ROWS],
        dma((4,)),
        dma((4,)),
        dma((2,)),
        dma((2,)),
        dma((2,)),
        dma((2, 2)),
        dma((2, len(CHUNK_ROWS))),
        dma((2, len(CHUNK_ROWS))),
    ]

    pre, w2g = pl.pallas_call(
        kernel,
        out_shape=(
            pltpu.VMEM((CH, 8, LANES), BF16),
            pltpu.VMEM((TAPS, 4, FILT), F32),
        ),
        in_specs=[hbm] * 5,
        out_specs=(vmem, vmem),
        scratch_shapes=scratch,
        compiler_params=pltpu.CompilerParams(
            collective_id=0, has_side_effects=True, vmem_limit_bytes=60 * 1024 * 1024
        ),
        name="layers",
    )(
        volumes[0],
        jnp.transpose(w_first),
        bias_first.reshape(1, CH),
        jnp.transpose(w_second, (1, 0, 2)),
        cotangent[0],
    )
    pre, w2g = pl.pallas_call(
        hand_over,
        out_shape=(
            jax.ShapeDtypeStruct(pre.shape, pre.dtype),
            jax.ShapeDtypeStruct(w2g.shape, w2g.dtype),
        ),
        in_specs=[vmem, vmem],
        out_specs=(hbm, hbm),
        scratch_shapes=[dma((2,))],
        name="hand_over",
    )(
        pltpu.with_memory_space_constraint(pre, pltpu.VMEM),
        pltpu.with_memory_space_constraint(w2g, pltpu.VMEM),
    )
    return pre.reshape(1, CH, 2, 4, LANES), jnp.transpose(w2g, (2, 0, 1))


def solution(mesh):
    placed = (P("samp", None, "grp", None, None), P(), P(), P(), P("samp", "grp", None, None))
    return jax.shard_map(
        on_device,
        mesh=mesh,
        in_specs=placed,
        out_specs=(P("samp", None, "grp", None, None), P(None, None, "grp")),
        check_vma=False,
    )
```
